256 devices in a mesh: row: 16 (over y, z_hi), col: 16 (over x, z_lo, core).
Axes of the slice: x: 4, y: 4, z: 8 (z_hi: 4, z_lo: 2; z = z_hi * 2 + z_lo), core: 2. Of those that a mesh axis runs over, the one named last changes fastest.
Arguments:
- features: bfloat16 [65536, 512], P(('row', 'col')), may hold values from -8 to 8
- w_self: bfloat16 [512, 512], replicated, may hold values from -0.25 to 0.25
- w_neigh: bfloat16 [512, 512], replicated, may hold values from -0.25 to 0.25
- cotangent: bfloat16 [65536, 512], P(('row', 'col')), may hold values from -8 to 8
- tile_values: bfloat16 [12288, 256, 256], P(('row', 'col')), as said below
- tile_dst: int32 [12288], P(('row', 'col')), may hold values from 0 to 15
- tile_src: int32 [12288], P(('row', 'col')), may hold values from 0 to 15
- tile_count: int32 [256], P(('row', 'col')), may hold values from 1 to 47, as said below
Outputs:
- output: bfloat16 [65536, 512], P(('row', 'col'))
- grad_features: bfloat16 [65536, 512], P(('row', 'col'))
- grad_self: float32 [512, 512], replicated
- grad_neigh: float32 [512, 512], replicated
The draws below stay inside these ranges and needn't reach their ends.
Inputs may be any that keep to these rules, and one draw needn't show every extreme that they name: `tile_count`: A is symmetric: a live slot at tiles (I, J) has a live slot at (J, I) with the transposed values, and each device's diagonal tile of its own node block (I = J = d) is live. Live slots come first, each (a, b) once; the busiest device has exactly 47 live slots. `tile_values`: entries are nonnegative; the diagonal of every node's own diagonal tile is 1 or more.
All inputs are finite; a program needn't handle non-finite values.
Results may differ from the reference program's by a relative error of at most 0.0085.
Values may be sent and summed in bfloat16 or wider, within the bound.
No kernel may reach another device: no remote copies, remote signals or barrier semaphores. Data moves between devices by JAX's collectives and lax.ppermute only.
A program may use at most 128 MiB of HBM per device.

```python
import math
import jax
import jax.numpy as jnp
from jax import lax

F = 512
TILE = 256
TILES_DEV = 48
REACH = 23
NODES = 65536
N_COL = 16
DEVICES = 256


def layout(key):
    ordering = jax.random.permutation(jax.random.fold_in(key, 11), DEVICES).astype(jnp.int32)
    places = jnp.arange(DEVICES, dtype=jnp.int32)
    position = jnp.zeros((DEVICES,), jnp.int32).at[ordering].set(places)
    rolled = jax.random.randint(jax.random.fold_in(key, 12), (DEVICES,), 0, REACH + 1).astype(jnp.int32)
    lower = REACH // 8
    base_reach = lower + rolled * rolled * (REACH - lower) // max(REACH * REACH, 1)
    distance = jnp.minimum(places, DEVICES - places)
    reach_at = jnp.where(distance == 0, REACH, jnp.maximum(base_reach, jnp.where(distance <= REACH, distance, 0)))
    offsets = jnp.arange(-REACH, REACH + 1, dtype=jnp.int32)
    home = position[:, None]
    neighbor_pos = (home + offsets[None, :]) % DEVICES
    partner = ordering[neighbor_pos]
    kept_mask = jnp.abs(offsets)[None, :] <= jnp.minimum(reach_at[home], reach_at[neighbor_pos])
    number = jnp.sum(kept_mask.astype(jnp.int32), axis=1).astype(jnp.int32)
    arranged = jnp.argsort(1 - kept_mask.astype(jnp.int32), axis=1, stable=True)
    partner = jnp.take_along_axis(partner, arranged, axis=1)
    kept_sorted = jnp.take_along_axis(kept_mask, arranged, axis=1)
    own = places[:, None]
    partner = jnp.where(kept_sorted, partner, own)
    partner = jnp.concatenate([partner, own], axis=1)
    return ((partner % N_COL).astype(jnp.int32), (partner // N_COL).astype(jnp.int32), number)


def band_angle(key):
    ordering = jax.random.permutation(jax.random.fold_in(key, 11), DEVICES).astype(jnp.int32)
    places = jnp.arange(DEVICES, dtype=jnp.int32)
    position = jnp.zeros((DEVICES,), jnp.int32).at[ordering].set(places)
    return position.astype(jnp.float32) * (2.0 * math.pi / DEVICES)


def smooth_field(key, angle, decay):
    harmonics = max(2, DEVICES // (REACH + 1))
    total_weight = math.sqrt(sum((float(h) ** (-2.0 * decay) for h in range(1, harmonics + 1))))
    field = jnp.zeros((DEVICES, F), jnp.float32)
    for h in range(1, harmonics + 1):
        harmonic_key = jax.random.fold_in(key, h)
        cos_coeff = jax.random.normal(jax.random.fold_in(harmonic_key, 0), (F,), jnp.float32)
        sin_coeff = jax.random.normal(jax.random.fold_in(harmonic_key, 1), (F,), jnp.float32)
        weight = float(h) ** (-decay) / total_weight
        field = field + weight * (jnp.cos(h * angle)[:, None] * cos_coeff[None, :] + jnp.sin(h * angle)[:, None] * sin_coeff[None, :])
    return jnp.repeat(field, TILE, axis=0)


def draw_features(key, part):
    angle = band_angle(key)
    key = jax.random.fold_in(key, 31)
    shared = smooth_field(jax.random.fold_in(key, 1), angle, 1.0)
    noise = jax.random.normal(jax.random.fold_in(key, 2), (NODES, F), jnp.float32)
    values = 0.7 * shared + noise
    return jnp.clip(values, -8.0, 8.0).astype(jnp.bfloat16)


def draw_cotangent(key, part):
    angle = band_angle(key)
    key = jax.random.fold_in(key, 37)
    shared = smooth_field(jax.random.fold_in(key, 1), angle, 1.0)
    noise = jax.random.normal(jax.random.fold_in(key, 2), (NODES, F), jnp.float32)
    values = 0.7 * shared + noise
    return jnp.clip(values, -8.0, 8.0).astype(jnp.bfloat16)


def draw_tile_dst(key, part):
    dest_index, source_index, number = layout(key)
    return dest_index.reshape(-1)


def draw_tile_src(key, part):
    dest_index, source_index, number = layout(key)
    return source_index.reshape(-1)


def draw_tile_count(key, part):
    dest_index, source_index, number = layout(key)
    return number


def pair_tile(key, pair_id, first, second, bottom, log_top):
    pair_key = jax.random.fold_in(key, pair_id)
    density = min(1.0, 4.0 / TILE)
    entries = jax.random.uniform(pair_key, (TILE, TILE), jnp.float32, bottom, 1.0)
    kept = jax.random.bernoulli(jax.random.fold_in(pair_key, 2), density, (TILE, TILE))
    entries = jnp.where(kept, entries, 0.0)
    self_weight = jax.random.uniform(jax.random.fold_in(pair_key, 3), (TILE,), jnp.float32, 1.0, 2.0)
    spread = jnp.exp(jax.random.uniform(jax.random.fold_in(pair_key, 1), (), jnp.float32, 0.0, log_top))
    swapped = entries.T
    diagonal_block = 0.5 * (entries + swapped) + jnp.diag(self_weight)
    block_values = jnp.where(first < second, entries, jnp.where(first > second, swapped, diagonal_block))
    return block_values * spread


def draw_tile_values(key, part):
    dest_index, source_index, number = layout(key)
    key = jax.random.fold_in(key, 5)
    devices = jnp.arange(DEVICES, dtype=jnp.int32)[:, None]
    row_tile = devices // N_COL * N_COL + dest_index
    col_tile = source_index * N_COL + devices % N_COL
    pair_ids = jnp.minimum(row_tile, col_tile) * DEVICES + jnp.maximum(row_tile, col_tile)
    bottom = 0.05
    log_top = math.log(10.0)
    values = jax.vmap(lambda pair_id, first, second: pair_tile(key, pair_id, first, second, bottom, log_top))(pair_ids.reshape(-1), row_tile.reshape(-1), col_tile.reshape(-1))
    return values.astype(jnp.bfloat16)


def gaussian(key, extent, scale, limit, kind=jnp.bfloat16):
    values = scale * jax.random.normal(key, extent, jnp.float32)
    return jnp.clip(values, min=-limit, max=limit).astype(kind)


def setup_inputs(seed: int = 0) -> dict:
    keys = jax.random.split(jax.random.key(seed), 9)
    features = draw_features(jax.random.fold_in(keys[8], 71), 0)
    w_self = gaussian(keys[1], (F, F), F ** -0.5, 0.25)
    w_neigh = gaussian(keys[2], (F, F), F ** -0.5, 0.25)
    cotangent = draw_cotangent(jax.random.fold_in(keys[8], 71), 0)
    tile_values = draw_tile_values(jax.random.fold_in(keys[8], 71), 0)
    tile_dst = draw_tile_dst(jax.random.fold_in(keys[8], 71), 0)
    tile_src = draw_tile_src(jax.random.fold_in(keys[8], 71), 0)
    tile_count = draw_tile_count(jax.random.fold_in(keys[8], 71), 0)
    return {"features": features, "w_self": w_self, "w_neigh": w_neigh, "cotangent": cotangent, "tile_values": tile_values, "tile_dst": tile_dst, "tile_src": tile_src, "tile_count": tile_count}


def reference(features, w_self, w_neigh, cotangent, tile_values, tile_dst, tile_src, tile_count):
    feature_tiles = features.reshape(DEVICES, TILE, F)
    tile_grid = tile_values.reshape(DEVICES, TILES_DEV, TILE, TILE)
    dest_index = tile_dst.reshape(DEVICES, TILES_DEV)
    source_index = tile_src.reshape(DEVICES, TILES_DEV)
    slot_ids = jnp.arange(TILES_DEV, dtype=jnp.int32)

    def placing(device):
        device_row = device // N_COL
        device_col = device % N_COL
        row_tile = (device_row * N_COL + dest_index[device]).astype(jnp.int32)
        col_tile = (source_index[device] * N_COL + device_col).astype(jnp.int32)
        active = (slot_ids < tile_count[device]).astype(jnp.float32)
        return row_tile, col_tile, active

    def forward_step(carry, device):
        accumulated, degree = carry
        row_tile, col_tile, active = placing(device)
        tile_block = tile_grid[device].astype(jnp.float32)
        source_rows = feature_tiles[col_tile].astype(jnp.float32)
        product = jnp.einsum('tij,tjf->tif', tile_block, source_rows) * active[:, None, None]
        accumulated = accumulated.at[row_tile].add(product)
        degree = degree.at[row_tile].add(jnp.sum(tile_block, axis=2) * active[:, None])
        return (accumulated, degree), None

    start_carry = (jnp.zeros((DEVICES, TILE, F), jnp.float32), jnp.zeros((DEVICES, TILE), jnp.float32))
    (accumulated, degree), _ = lax.scan(forward_step, start_carry, jnp.arange(DEVICES, dtype=jnp.int32))
    summed = accumulated.reshape(NODES, F)
    degree = degree.reshape(NODES)
    neighbor_mean = (summed / degree[:, None]).astype(jnp.bfloat16)
    preact = jnp.dot(features, w_self, preferred_element_type=jnp.float32) + jnp.dot(neighbor_mean, w_neigh, preferred_element_type=jnp.float32)
    sigmoid_part = jax.nn.sigmoid(preact)
    output = (preact * sigmoid_part).astype(jnp.bfloat16)
    grad_pre = (cotangent.astype(jnp.float32) * sigmoid_part * (1.0 + preact * (1.0 - sigmoid_part))).astype(jnp.bfloat16)
    grad_self = jnp.dot(features.T, grad_pre, preferred_element_type=jnp.float32)
    grad_neigh = jnp.dot(neighbor_mean.T, grad_pre, preferred_element_type=jnp.float32)
    scaled_back = (jnp.dot(grad_pre, w_neigh.T, preferred_element_type=jnp.float32) / degree[:, None]).astype(jnp.bfloat16)
    scaled_tiles = scaled_back.reshape(DEVICES, TILE, F)

    def backward_step(accumulated, device):
        row_tile, col_tile, active = placing(device)
        tile_block = tile_grid[device].astype(jnp.float32)
        source_rows = scaled_tiles[row_tile].astype(jnp.float32)
        product = jnp.einsum('tji,tjf->tif', tile_block, source_rows) * active[:, None, None]
        return accumulated.at[col_tile].add(product), None

    returned, _ = lax.scan(backward_step, jnp.zeros((DEVICES, TILE, F), jnp.float32), jnp.arange(DEVICES, dtype=jnp.int32))
    grad_features = (jnp.dot(grad_pre, w_self.T, preferred_element_type=jnp.float32) + returned.reshape(NODES, F)).astype(jnp.bfloat16)
    return (output, grad_features, grad_self, grad_neigh)
```

```python
import functools

import jax
import jax.numpy as jnp
from jax import lax
from jax.experimental import pallas as pl
from jax.experimental.pallas import tpu as pltpu
from jax.sharding import PartitionSpec as P

MIB = 1 << 20
BOTH = ("row", "col")
CONTRACT_ROWS = (((0,), (0,)), ((), ()))
CONTRACT_COLS = (((1,), (1,)), ((), ()))

GATHER = (
    (("z", 1, 3), ("z", 3, 1), ("y", 1, 3), ("y", 3, 1)),
    (("y", 1, 3), ("y", 3, 1), ("z", 1, 3), ("z", 3, 1)),
)
ROWS = ((0, 176), (176, 80))
REDUCE = (
    (("x", 1, 3), ("x", 3, 1), ("l", 1, 1)),
    (("l", 1, 1), ("x", 1, 3), ("x", 3, 1)),
)
ROW_SUM = (("y", 1, 3), ("y", 3, 1), ("z", 1, 3), ("z", 3, 1))
AXES = ("y", "z", "x", "l", "c")
SIZES = (4, 4, 4, 2, 2)


def exchange(value, step):
    axis, *masks = step
    pairs = []
    for i in range(256):
        at, rest = {}, i
        for name, size in zip(reversed(AXES), reversed(SIZES)):
            at[name], rest = rest % size, rest // size
        at[axis] ^= masks[at["c"]]
        j = 0
        for name, size in zip(AXES, SIZES):
            j = j * size + at[name]
        pairs.append((i, j))
    return lax.ppermute(value, BOTH, pairs)


def swap(value):
    return exchange(value, ("c", 1, 1))


def place(info, steps, bits, core=None):
    at = {name: info[k] for k, name in enumerate(AXES)}
    core = info[4] if core is None else core
    for step, bit in zip(steps, bits):
        if bit:
            axis, first, second = step
            at[axis] = lax.bitwise_xor(at[axis], first + core * (second - first))
    return at


def params(limit):
    return pltpu.CompilerParams(vmem_limit_bytes=limit * MIB)


VMEM = pl.BlockSpec(memory_space=pltpu.VMEM)
SMEM = pl.BlockSpec(memory_space=pltpu.SMEM)
ANY = pl.BlockSpec(memory_space=pl.ANY)


def chip_slots(info, steps, core=None):
    chips = []
    for s in range(8):
        at = place(info, steps, (s >> 2 & 1, s >> 1 & 1, s & 1), core)
        chips.append(at["x"] * 2 + at["l"])
    return chips


def degree_kernel(info, index, tiles, own, other, acc, buf, sem):
    count, core = index[96], info[4]

    def begin(s, carry):
        pltpu.make_async_copy(tiles.at[s], buf.at[s], sem.at[s]).start()
        return carry

    lax.fori_loop(0, count, begin, 0)
    acc[...] = jnp.zeros_like(acc)
    ones = jnp.ones((8, buf.shape[1]), jnp.bfloat16)

    def visit(s, carry):
        pltpu.make_async_copy(tiles.at[s], buf.at[s], sem.at[s]).wait()
        acc[index[s]] += lax.dot_general(
            ones, buf[s], CONTRACT_COLS, preferred_element_type=jnp.float32
        )
        return carry

    lax.fori_loop(0, count, visit, 0)
    for s, chip in enumerate(chip_slots(info, REDUCE[0])):
        own[s] = acc[chip * 2 + core]
    for s, chip in enumerate(chip_slots(info, REDUCE[0], 1 - core)):
        other[s] = acc[chip * 2 + 1 - core]


def partial_degree(info, index, tiles):
    slots, edge, _ = tiles.shape
    return pl.pallas_call(
        degree_kernel,
        out_shape=[jax.ShapeDtypeStruct((8, 8, edge), jnp.float32)] * 2,
        in_specs=[SMEM, SMEM, ANY],
        out_specs=[VMEM] * 2,
        scratch_shapes=[
            pltpu.VMEM((16, 8, edge), jnp.float32),
            pltpu.VMEM((slots, edge, edge), jnp.bfloat16),
            pltpu.SemaphoreType.DMA((slots,)),
        ],
        compiler_params=params(16),
        name="degree",
    )(info, index, tiles)


def degree_stages(info, index, tiles):
    def begin(state):
        own, other = partial_degree(info, index, tiles)
        return own + swap(other)

    def add(total):
        for step, n in zip(REDUCE[0], (4, 2, 1)):
            total = total[:n] + exchange(total[n:], step)
        return total

    return (None, None, begin, add)


def spread_kernel(info, index0, index1, tiles0, tiles1, *refs):
    pieces, (send0, keep0, send1, keep1, x, acc, buf, sem, piece_sem) = refs[:4], refs[4:]
    core = info[4]
    slots = tiles0.shape[0]

    copies = []
    for chain, (steps, (first, rows)) in enumerate(zip(GATHER, ROWS)):
        for s in range(16):
            at = place(info, steps, (s & 1, s >> 1 & 1, s >> 2 & 1, s >> 3))
            block = at["y"] * 4 + at["z"]
            copies.append(
                pltpu.make_async_copy(
                    pieces[chain * 2 + s // 8].at[s % 8],
                    x.at[pl.ds(block * 2, 2), pl.ds(first, rows), :],
                    piece_sem.at[chain, s],
                )
            )
    for copy in copies:
        copy.start()

    def tile_copy(tiles, base, s):
        return pltpu.make_async_copy(tiles.at[s], buf.at[base + s], sem.at[base + s])

    work = ((index0, tiles0, 0), (index1, tiles1, 1))
    for index, tiles, rel in work:

        def begin(s, carry, tiles=tiles, base=rel * slots):
            tile_copy(tiles, base, s).start()
            return carry

        lax.fori_loop(0, index[96], begin, 0)
    acc[...] = jnp.zeros_like(acc)
    for copy in copies:
        copy.wait()
    for index, tiles, rel in work:

        def visit(s, carry, index=index, tiles=tiles, rel=rel):
            tile_copy(tiles, rel * slots, s).wait()
            acc[index[s]] += jnp.dot(
                buf[rel * slots + s],
                x[index[48 + s] * 2 + rel],
                preferred_element_type=jnp.float32,
            )
            return carry

        lax.fori_loop(0, index[96], visit, 0)
    for chain, (send, keep) in enumerate(((send0, keep0), (send1, keep1))):
        cols = slice(chain * 128, chain * 128 + 128)
        for s, chip in enumerate(chip_slots(info, REDUCE[chain])):
            for rel in range(2):
                block = chip * 2 + (core if rel == 0 else 1 - core)
                if s < 4:
                    keep[s, rel] = acc[block, :, cols]
                else:
                    send[s - 4, rel] = acc[block, :, cols].astype(jnp.bfloat16)


def spread(info, work, pieces):
    (index0, tiles0), (index1, tiles1) = work
    slots, edge, _ = tiles0.shape
    quarter = (4, 2, edge, 128)
    return pl.pallas_call(
        spread_kernel,
        out_shape=[
            jax.ShapeDtypeStruct(quarter, jnp.bfloat16),
            jax.ShapeDtypeStruct(quarter, jnp.float32),
        ]
        * 2,
        in_specs=[SMEM] * 3 + [ANY] * 6,
        out_specs=[VMEM] * 4,
        scratch_shapes=[
            pltpu.VMEM((32, edge, 256), jnp.bfloat16),
            pltpu.VMEM((16, edge, 256), jnp.float32),
            pltpu.VMEM((2 * slots, edge, edge), jnp.bfloat16),
            pltpu.SemaphoreType.DMA((2 * slots,)),
            pltpu.SemaphoreType.DMA((2, 16)),
        ],
        compiler_params=params(36),
        cost_estimate=pl.CostEstimate(
            flops=2 * 47 * edge * edge * 512, bytes_accessed=20 * MIB, transcendentals=0
        ),
        name="spread",
    )(info, index0, index1, tiles0, tiles1, *pieces)


def join_kernel(keep, got, send, rest):
    n = rest.shape[0]
    for s in range(2 * n):
        total = keep[s] + got[s].astype(jnp.float32)
        if s < n:
            rest[s] = total
        else:
            send[s - n] = total.astype(jnp.bfloat16)


def join(keep, got):
    shape = (keep.shape[0] // 2,) + keep.shape[1:]
    return pl.pallas_call(
        join_kernel,
        out_shape=[
            jax.ShapeDtypeStruct(shape, jnp.bfloat16),
            jax.ShapeDtypeStruct(shape, jnp.float32),
        ],
        in_specs=[VMEM] * 2,
        out_specs=[VMEM] * 2,
        compiler_params=params(16),
        name="join",
    )(keep, got)


def last_join_kernel(keep0, got0, keep1, got1, own, other):
    for chain, (keep, got) in enumerate(((keep0, got0), (keep1, got1))):
        cols = slice(chain * 128, chain * 128 + 128)
        own[:, cols] = keep[0, 0] + got[0, 0].astype(jnp.float32)
        other[:, cols] = keep[0, 1] + got[0, 1].astype(jnp.float32)


def last_join(keep0, got0, keep1, got1):
    edge = keep0.shape[2]
    return pl.pallas_call(
        last_join_kernel,
        out_shape=[jax.ShapeDtypeStruct((edge, 256), jnp.float32)] * 2,
        in_specs=[VMEM] * 4,
        out_specs=[VMEM] * 2,
        compiler_params=params(16),
        name="last_join",
    )(keep0, got0, keep1, got1)


def aggregate(info, work, own_half, other_half, stages, state):
    arrived = swap(other_half)
    pair = jnp.stack([own_half, arrived])
    have = [pair[None, :, first : first + rows] for first, rows in ROWS]
    for k in range(4):
        got = [exchange(h, steps[k]) for h, steps in zip(have, GATHER)]
        if stages[k] is not None:
            state = stages[k](state)
            got, state = lax.optimization_barrier((got, state))
        if k < 3:
            have = [jnp.concatenate([h, g]) for h, g in zip(have, got)]
            have = lax.optimization_barrier(have)
    send0, keep0, send1, keep1 = spread(info, work, (have[0], got[0], have[1], got[1]))
    send, keep = [send0, send1], [keep0, keep1]
    for k in range(2):
        arrived = [exchange(send[chain], REDUCE[chain][k]) for chain in range(2)]
        arrived = lax.optimization_barrier(arrived)
        for chain in range(2):
            send[chain], keep[chain] = join(keep[chain], arrived[chain])
    arrived = [exchange(send[chain], REDUCE[chain][2]) for chain in range(2)]
    own, other = last_join(keep[0], arrived[0], keep[1], arrived[1])
    return own, swap(other), state


def whole_width(core, own, got):
    first = core == 0
    return jnp.concatenate([jnp.where(first, own, got), jnp.where(first, got, own)], axis=1)


def dense_kernel(
    info, features, cotangent, w_self, w_neigh, degree, own, got, output, grad_pre, mean, mine, theirs
):
    deg = degree[:, 0:1]
    core = info[4]
    summed = whole_width(core, own[...], got[...])
    neighbor_mean = (summed / deg).astype(jnp.bfloat16)
    mean[...] = neighbor_mean
    preact = jnp.dot(features[...], w_self[...], preferred_element_type=jnp.float32) + jnp.dot(
        neighbor_mean, w_neigh[...], preferred_element_type=jnp.float32
    )
    part = jax.nn.sigmoid(preact)
    output[...] = (preact * part).astype(jnp.bfloat16)
    grad = (
        cotangent[...].astype(jnp.float32) * part * (1.0 + preact * (1.0 - part))
    ).astype(jnp.bfloat16)
    grad_pre[...] = grad
    back = (
        lax.dot_general(grad, w_neigh[...], CONTRACT_COLS, preferred_element_type=jnp.float32)
        / deg
    )
    mine[...] = jnp.where(core == 0, back[:, :256], back[:, 256:]).astype(jnp.bfloat16)
    theirs[...] = jnp.where(core == 0, back[:, 256:], back[:, :256]).astype(jnp.bfloat16)


def dense(info, features, cotangent, w_self, w_neigh, degree, own, got):
    nodes, width = features.shape
    full = jax.ShapeDtypeStruct((nodes, width), jnp.bfloat16)
    half = jax.ShapeDtypeStruct((nodes, 256), jnp.bfloat16)
    return pl.pallas_call(
        dense_kernel,
        out_shape=[full] * 3 + [half] * 2,
        in_specs=[SMEM] + [VMEM] * 7,
        out_specs=[VMEM] * 5,
        compiler_params=params(24),
        name="dense",
    )(info, features, cotangent, w_self, w_neigh, degree, own, got)


def weights_kernel(info, features, mean, grad_pre, w_self, keep, send, own):
    grad = grad_pre[...]
    grad_self = lax.dot_general(
        features[...], grad, CONTRACT_ROWS, preferred_element_type=jnp.float32
    )
    grad_neigh = lax.dot_general(
        mean[...], grad, CONTRACT_ROWS, preferred_element_type=jnp.float32
    )
    first = info[4] == 0
    keep[...] = jnp.where(first, grad_self, grad_neigh)
    send[...] = jnp.where(first, grad_neigh, grad_self)
    own[...] = lax.dot_general(
        grad, w_self[...], CONTRACT_COLS, preferred_element_type=jnp.float32
    )


def weights(info, features, mean, grad_pre, w_self):
    nodes, width = features.shape
    square = jax.ShapeDtypeStruct((width, width), jnp.float32)
    return pl.pallas_call(
        weights_kernel,
        out_shape=[square, square, jax.ShapeDtypeStruct((nodes, width), jnp.float32)],
        in_specs=[SMEM] + [VMEM] * 4,
        out_specs=[VMEM] * 3,
        compiler_params=params(24),
        name="weights",
    )(info, features, mean, grad_pre, w_self)


def weight_blocks_kernel(info, keep, got, send, rest):
    for s, chip in enumerate(chip_slots(info, REDUCE[0])):
        rows = pl.ds(pl.multiple_of(chip * 64, 64), 64)
        total = keep[rows, :] + got[rows, :]
        if s < 4:
            rest[s] = total
        else:
            send[s - 4] = total


def weight_blocks(info, keep, got):
    shape = jax.ShapeDtypeStruct((4, 64, keep.shape[1]), jnp.float32)
    return pl.pallas_call(
        weight_blocks_kernel,
        out_shape=[shape] * 2,
        in_specs=[SMEM, VMEM, VMEM],
        out_specs=[VMEM] * 2,
        compiler_params=params(16),
        name="weight_blocks",
    )(info, keep, got)


def weight_stages(info, features, w_self):
    steps = REDUCE[0]

    def local(state):
        grad_pre, mean = state
        keep, send, own_term = weights(info, features, mean, grad_pre, w_self)
        return keep, swap(send), own_term

    def first(state):
        keep, got, own_term = state
        send, rest = weight_blocks(info, keep, got)
        return rest + exchange(send, steps[0]), own_term

    def middle(state):
        total, own_term = state
        total = total[:2] + exchange(total[2:], steps[1])
        return total[0] + exchange(total[1], steps[2]), own_term

    def last(state):
        total, own_term = state
        for step in ROW_SUM:
            total = total + exchange(total, step)
        return total, own_term

    return (local, first, middle, last)


def split_weights(total):
    every = lax.all_gather(total, "col", axis=0, tiled=False)
    width = total.shape[1]
    both = every.reshape(8, 2, 64, width)
    return both[:, 0].reshape(-1, width), both[:, 1].reshape(-1, width)


def finish_kernel(info, own_term, own, got, out):
    out[...] = (own_term[...] + whole_width(info[4], own[...], got[...])).astype(jnp.bfloat16)


def finish(info, own_term, own, got):
    return pl.pallas_call(
        finish_kernel,
        out_shape=jax.ShapeDtypeStruct(own_term.shape, jnp.bfloat16),
        in_specs=[SMEM] + [VMEM] * 3,
        out_specs=VMEM,
        compiler_params=params(16),
        name="finish",
    )(info, own_term, own, got)


def shards(features, w_self, w_neigh, cotangent, tile_values, tile_dst, tile_src, tile_count):
    row, col = lax.axis_index("row"), lax.axis_index("col")
    core = col % 2
    info = jnp.stack([row // 4, row % 4, col // 4, col // 2 % 2, core]).astype(jnp.int32)
    index = jnp.concatenate([tile_dst, tile_src, tile_count])
    work = ((index, tile_values), (swap(index), swap(tile_values)))

    first = core == 0
    mine = jnp.where(first, features[:, :256], features[:, 256:])
    theirs = jnp.where(first, features[:, 256:], features[:, :256])
    own, got, degree = aggregate(
        info, work, mine, theirs, degree_stages(info, index, tile_values), None
    )
    degree = jnp.broadcast_to(degree[0, 0][:, None], (degree.shape[-1], 128))
    output, grad_pre, mean, mine, theirs = dense(
        info, features, cotangent, w_self, w_neigh, degree, own, got
    )
    own, got, (total, own_term) = aggregate(
        info, work, mine, theirs, weight_stages(info, features, w_self), (grad_pre, mean)
    )
    grad_self, grad_neigh = split_weights(total)
    grad_features = finish(info, own_term, own, got)
    return (output, grad_features, grad_self, grad_neigh)


def solution(mesh):
    return jax.shard_map(
        shards,
        mesh=mesh,
        in_specs=(
            P(("row", "col"), None),
            P(),
            P(),
            P(("row", "col"), None),
            P(("row", "col"), None, None),
            P(("row", "col")),
            P(("row", "col")),
            P(("row", "col")),
        ),
        out_specs=(P(("row", "col"), None), P(("row", "col"), None), P(), P()),
        check_vma=False,
    )
```

```python
import functools

import jax
import jax.numpy as jnp
from jax import lax
from jax.experimental import pallas as pl
from jax.experimental.pallas import tpu as pltpu
from jax.sharding import PartitionSpec as P

MIB = 1 << 20
UNROLL = 4
BOTH = ("row", "col")
CONTRACT_ROWS = (((0,), (0,)), ((), ()))
CONTRACT_COLS = (((1,), (1,)), ((), ()))

GATHER = (
    (("z", 1, 3), ("z", 3, 1), ("y", 1, 3), ("y", 3, 1)),
    (("y", 1, 3), ("y", 3, 1), ("z", 1, 3), ("z", 3, 1)),
)
ROWS = ((0, 176), (176, 80))
REDUCE = (
    (("x", 1, 3), ("x", 3, 1), ("l", 1, 1)),
    (("l", 1, 1), ("x", 1, 3), ("x", 3, 1)),
)
ROW_SUM = (("y", 1, 3), ("y", 3, 1), ("z", 1, 3), ("z", 3, 1))
AXES = ("y", "z", "x", "l", "c")
SIZES = (4, 4, 4, 2, 2)


def exchange(value, step):
    axis, *masks = step
    pairs = []
    for i in range(256):
        at, rest = {}, i
        for name, size in zip(reversed(AXES), reversed(SIZES)):
            at[name], rest = rest % size, rest // size
        at[axis] ^= masks[at["c"]]
        j = 0
        for name, size in zip(AXES, SIZES):
            j = j * size + at[name]
        pairs.append((i, j))
    return lax.ppermute(value, BOTH, pairs)


def swap(value):
    return exchange(value, ("c", 1, 1))


def place(info, steps, bits, core=None):
    at = {name: info[k] for k, name in enumerate(AXES)}
    core = info[4] if core is None else core
    for step, bit in zip(steps, bits):
        if bit:
            axis, first, second = step
            at[axis] = lax.bitwise_xor(at[axis], first + core * (second - first))
    return at


def params(limit):
    return pltpu.CompilerParams(vmem_limit_bytes=limit * MIB)


VMEM = pl.BlockSpec(memory_space=pltpu.VMEM)
SMEM = pl.BlockSpec(memory_space=pltpu.SMEM)
ANY = pl.BlockSpec(memory_space=pl.ANY)


def chip_slots(info, steps, core=None):
    chips = []
    for s in range(8):
        at = place(info, steps, (s >> 2 & 1, s >> 1 & 1, s & 1), core)
        chips.append(at["x"] * 2 + at["l"])
    return chips


def degree_kernel(info, index, tiles, own, other, acc):
    count, core = index[96], info[4]
    acc[...] = jnp.zeros_like(acc)

    def add(s):
        values = tiles[s].astype(jnp.float32)
        acc[index[s]] += values[:, :128] + values[:, 128:]

    def several(group, carry):
        for k in range(UNROLL):
            add(group * UNROLL + k)
        return carry

    def single(s, carry):
        add(s)
        return carry

    groups = lax.div(count, UNROLL)
    lax.fori_loop(0, groups, several, 0)
    lax.fori_loop(groups * UNROLL, count, single, 0)

    def sums(block):
        total = jnp.sum(jnp.transpose(acc[block]), axis=0, keepdims=True)
        return jnp.broadcast_to(total, (8, total.shape[1]))

    for s, chip in enumerate(chip_slots(info, REDUCE[0])):
        own[s] = sums(chip * 2 + core)
    for s, chip in enumerate(chip_slots(info, REDUCE[0], 1 - core)):
        other[s] = sums(chip * 2 + 1 - core)


def partial_degree(info, index, tiles):
    edge = tiles.shape[1]
    return pl.pallas_call(
        degree_kernel,
        out_shape=[jax.ShapeDtypeStruct((8, 8, edge), jnp.float32)] * 2,
        in_specs=[SMEM, SMEM, VMEM],
        out_specs=[VMEM] * 2,
        scratch_shapes=[
            pltpu.VMEM((16, edge, 128), jnp.float32),
        ],
        compiler_params=params(16),
        name="degree",
    )(info, index, tiles)


def degree_stages(info, index, tiles):
    def begin(state):
        own, other = partial_degree(info, index, tiles)
        return own + swap(other)

    def add(total, part):
        for step, n in part:
            total = total[:n] + exchange(total[n:], step)
        return total

    parts = list(zip(REDUCE[0], (4, 2, 1)))
    return {
        1: begin,
        2: lambda total: add(total, parts[:2]),
        3: lambda total: add(total, parts[2:]),
    }


def spread_kernel(info, index0, index1, tiles0, tiles1, *refs):
    pieces, (send0, keep0, send1, keep1, x, acc, buf, sem, piece_sem) = refs[:4], refs[4:]
    core = info[4]
    slots = tiles0.shape[0]

    copies = []
    for chain, (steps, (first, rows)) in enumerate(zip(GATHER, ROWS)):
        for s in range(16):
            at = place(info, steps, (s & 1, s >> 1 & 1, s >> 2 & 1, s >> 3))
            block = at["y"] * 4 + at["z"]
            copies.append(
                pltpu.make_async_copy(
                    pieces[chain * 2 + s // 8].at[s % 8],
                    x.at[pl.ds(block * 2, 2), pl.ds(first, rows), :],
                    piece_sem.at[chain, s],
                )
            )
    for copy in copies:
        copy.start()

    def tile_copy(tiles, base, s):
        return pltpu.make_async_copy(tiles.at[s], buf.at[base + s], sem.at[base + s])

    work = ((index0, tiles0, 0), (index1, tiles1, 1))
    for index, tiles, rel in work:

        def begin(s, carry, tiles=tiles, base=rel * slots):
            tile_copy(tiles, base, s).start()
            return carry

        lax.fori_loop(0, index[96], begin, 0)
    acc[...] = jnp.zeros_like(acc)
    for copy in copies:
        copy.wait()
    for index, tiles, rel in work:

        def multiply(s, index=index, rel=rel):
            acc[index[s]] += jnp.dot(
                buf[rel * slots + s],
                x[index[48 + s] * 2 + rel],
                preferred_element_type=jnp.float32,
            )

        def several(group, carry, tiles=tiles, rel=rel, multiply=multiply):
            for k in range(UNROLL):
                tile_copy(tiles, rel * slots, group * UNROLL + k).wait()
            for k in range(UNROLL):
                multiply(group * UNROLL + k)
            return carry

        def single(s, carry, tiles=tiles, rel=rel, multiply=multiply):
            tile_copy(tiles, rel * slots, s).wait()
            multiply(s)
            return carry

        groups = lax.div(index[96], UNROLL)
        lax.fori_loop(0, groups, several, 0)
        lax.fori_loop(groups * UNROLL, index[96], single, 0)
    for chain, (send, keep) in enumerate(((send0, keep0), (send1, keep1))):
        part = pl.ds(ROWS[chain][0], ROWS[chain][1])
        for s, chip in enumerate(chip_slots(info, REDUCE[chain])):
            for rel in range(2):
                block = chip * 2 + (core if rel == 0 else 1 - core)
                if s < 4:
                    keep[s, rel] = acc[block, part, :]
                else:
                    send[s - 4, rel] = acc[block, part, :].astype(jnp.bfloat16)


def spread(info, work, pieces):
    (index0, tiles0), (index1, tiles1) = work
    slots, edge, _ = tiles0.shape
    return pl.pallas_call(
        spread_kernel,
        out_shape=[
            jax.ShapeDtypeStruct((4, 2, rows, 256), dtype)
            for _, rows in ROWS
            for dtype in (jnp.bfloat16, jnp.float32)
        ],
        in_specs=[SMEM] * 3 + [ANY] * 6,
        out_specs=[VMEM] * 4,
        scratch_shapes=[
            pltpu.VMEM((32, edge, 256), jnp.bfloat16),
            pltpu.VMEM((16, edge, 256), jnp.float32),
            pltpu.VMEM((2 * slots, edge, edge), jnp.bfloat16),
            pltpu.SemaphoreType.DMA((2 * slots,)),
            pltpu.SemaphoreType.DMA((2, 16)),
        ],
        compiler_params=params(60),
        cost_estimate=pl.CostEstimate(
            flops=2 * 47 * edge * edge * 512, bytes_accessed=20 * MIB, transcendentals=0
        ),
        name="spread",
    )(info, index0, index1, tiles0, tiles1, *pieces)


def join_kernel(keep, got, send, rest):
    n = rest.shape[0]
    for s in range(2 * n):
        total = keep[s] + got[s].astype(jnp.float32)
        if s < n:
            rest[s] = total
        else:
            send[s - n] = total.astype(jnp.bfloat16)


def join(keep, got):
    shape = (keep.shape[0] // 2,) + keep.shape[1:]
    return pl.pallas_call(
        join_kernel,
        out_shape=[
            jax.ShapeDtypeStruct(shape, jnp.bfloat16),
            jax.ShapeDtypeStruct(shape, jnp.float32),
        ],
        in_specs=[VMEM] * 2,
        out_specs=[VMEM] * 2,
        compiler_params=params(16),
        name="join",
    )(keep, got)


def last_join_kernel(keep0, got0, keep1, got1, own, other):
    for chain, (keep, got) in enumerate(((keep0, got0), (keep1, got1))):
        part = pl.ds(ROWS[chain][0], ROWS[chain][1])
        own[part, :] = keep[0, 0] + got[0, 0].astype(jnp.float32)
        other[part, :] = keep[0, 1] + got[0, 1].astype(jnp.float32)


def last_join(keep0, got0, keep1, got1):
    edge = keep0.shape[2] + keep1.shape[2]
    return pl.pallas_call(
        last_join_kernel,
        out_shape=[jax.ShapeDtypeStruct((edge, 256), jnp.float32)] * 2,
        in_specs=[VMEM] * 4,
        out_specs=[VMEM] * 2,
        compiler_params=params(16),
        name="last_join",
    )(keep0, got0, keep1, got1)


def aggregate(info, work, own_half, arrived, stages, state):
    def beside(k, values, state):
        if k not in stages:
            return values, state
        return lax.optimization_barrier((values, stages[k](state)))

    pair = jnp.stack([own_half, arrived])
    have = [pair[None, :, first : first + rows] for first, rows in ROWS]
    for k in range(4):
        got = [exchange(h, steps[k]) for h, steps in zip(have, GATHER)]
        got, state = beside(k, got, state)
        if k < 3:
            have = [jnp.concatenate([h, g]) for h, g in zip(have, got)]
            have = lax.optimization_barrier(have)
    parts = spread(info, work, (have[0], got[0], have[1], got[1]))
    parts, state = beside(4, parts, state)
    send, keep = [parts[0], parts[2]], [parts[1], parts[3]]
    for k in range(2):
        arrived = [exchange(send[chain], REDUCE[chain][k]) for chain in range(2)]
        arrived = lax.optimization_barrier(arrived)
        arrived, state = beside(5 + k, arrived, state)
        for chain in range(2):
            send[chain], keep[chain] = join(keep[chain], arrived[chain])
    arrived = [exchange(send[chain], REDUCE[chain][2]) for chain in range(2)]
    arrived, state = beside(7, arrived, state)
    own, other = last_join(keep[0], arrived[0], keep[1], arrived[1])
    return own, swap(other), state


def whole_width(core, own, got):
    first = core == 0
    return jnp.concatenate([jnp.where(first, own, got), jnp.where(first, got, own)], axis=1)


def dense_kernel(
    info, features, cotangent, w_self, w_neigh, degree, own, got, output, grad_pre, mean, mine, theirs
):
    deg = degree[:, 0:1]
    core = info[4]
    summed = whole_width(core, own[...], got[...])
    neighbor_mean = (summed / deg).astype(jnp.bfloat16)
    mean[...] = neighbor_mean
    preact = jnp.dot(features[...], w_self[...], preferred_element_type=jnp.float32) + jnp.dot(
        neighbor_mean, w_neigh[...], preferred_element_type=jnp.float32
    )
    part = jax.nn.sigmoid(preact)
    output[...] = (preact * part).astype(jnp.bfloat16)
    grad = (
        cotangent[...].astype(jnp.float32) * part * (1.0 + preact * (1.0 - part))
    ).astype(jnp.bfloat16)
    grad_pre[...] = grad
    back = (
        lax.dot_general(grad, w_neigh[...], CONTRACT_COLS, preferred_element_type=jnp.float32)
        / deg
    )
    mine[...] = jnp.where(core == 0, back[:, :256], back[:, 256:]).astype(jnp.bfloat16)
    theirs[...] = jnp.where(core == 0, back[:, 256:], back[:, :256]).astype(jnp.bfloat16)


def dense(info, features, cotangent, w_self, w_neigh, degree, own, got):
    nodes, width = features.shape
    full = jax.ShapeDtypeStruct((nodes, width), jnp.bfloat16)
    half = jax.ShapeDtypeStruct((nodes, 256), jnp.bfloat16)
    return pl.pallas_call(
        dense_kernel,
        out_shape=[full] * 3 + [half] * 2,
        in_specs=[SMEM] + [VMEM] * 7,
        out_specs=[VMEM] * 5,
        compiler_params=params(24),
        name="dense",
    )(info, features, cotangent, w_self, w_neigh, degree, own, got)


def weights_kernel(info, features, mean, grad_pre, w_self, keep, send, own):
    grad = grad_pre[...]
    grad_self = lax.dot_general(
        features[...], grad, CONTRACT_ROWS, preferred_element_type=jnp.float32
    )
    grad_neigh = lax.dot_general(
        mean[...], grad, CONTRACT_ROWS, preferred_element_type=jnp.float32
    )
    first = info[4] == 0
    keep[...] = jnp.where(first, grad_self, grad_neigh)
    send[...] = jnp.where(first, grad_neigh, grad_self)
    own[...] = lax.dot_general(
        grad, w_self[...], CONTRACT_COLS, preferred_element_type=jnp.float32
    )


def weights(info, features, mean, grad_pre, w_self):
    nodes, width = features.shape
    square = jax.ShapeDtypeStruct((width, width), jnp.float32)
    return pl.pallas_call(
        weights_kernel,
        out_shape=[square, square, jax.ShapeDtypeStruct((nodes, width), jnp.float32)],
        in_specs=[SMEM] + [VMEM] * 4,
        out_specs=[VMEM] * 3,
        compiler_params=params(24),
        name="weights",
    )(info, features, mean, grad_pre, w_self)


def weight_blocks_kernel(info, keep, got, send, rest):
    for s, chip in enumerate(chip_slots(info, REDUCE[0])):
        rows = pl.ds(pl.multiple_of(chip * 64, 64), 64)
        total = keep[rows, :] + got[rows, :]
        if s < 4:
            rest[s] = total
        else:
            send[s - 4] = total


def weight_blocks(info, keep, got):
    shape = jax.ShapeDtypeStruct((4, 64, keep.shape[1]), jnp.float32)
    return pl.pallas_call(
        weight_blocks_kernel,
        out_shape=[shape] * 2,
        in_specs=[SMEM, VMEM, VMEM],
        out_specs=[VMEM] * 2,
        compiler_params=params(16),
        name="weight_blocks",
    )(info, keep, got)


def weight_stages(info, features, w_self):
    steps = REDUCE[0]

    def local(state):
        grad_pre, mean = state
        keep, send, own_term = weights(info, features, mean, grad_pre, w_self)
        return keep, swap(send), own_term

    def first(state):
        keep, got, own_term = state
        send, rest = weight_blocks(info, keep, got)
        return rest + exchange(send, steps[0]), own_term

    def halve(step):
        def stage(state):
            total, own_term = state
            half = total.shape[0] // 2
            return total[:half] + exchange(total[half:], step), own_term

        return stage

    def row_sum(*chosen):
        def stage(state):
            total, own_term = state
            for step in chosen:
                total = total + exchange(total, step)
            return total, own_term

        return stage

    def collect(*chosen):
        def stage(state):
            total, own_term = state
            for step in chosen:
                total = jnp.concatenate([total, exchange(total, step)])
            return total, own_term

        return stage

    l_and_y = (halve(steps[2]), row_sum(ROW_SUM[0]))
    return {
        0: local,
        1: first,
        2: halve(steps[1]),
        3: lambda state: l_and_y[1](l_and_y[0](state)),
        4: row_sum(ROW_SUM[1]),
        5: row_sum(*ROW_SUM[2:]),
        6: collect(steps[2], steps[1]),
        7: collect(steps[0]),
    }


def both_weights_kernel(info, mine, theirs, grad_self, grad_neigh):
    core = info[4]
    for value, owner in ((mine, core), (theirs, 1 - core)):
        for s, chip in enumerate(chip_slots(info, REDUCE[0], owner)):
            rows = pl.ds(pl.multiple_of(chip * 64, 64), 64)

            @pl.when(owner == 0)
            def _(value=value, s=s, rows=rows):
                grad_self[rows, :] = value[s]

            @pl.when(owner == 1)
            def _(value=value, s=s, rows=rows):
                grad_neigh[rows, :] = value[s]


def both_weights(info, total):
    width = total.shape[2]
    return pl.pallas_call(
        both_weights_kernel,
        out_shape=[jax.ShapeDtypeStruct((8 * total.shape[1], width), jnp.float32)] * 2,
        in_specs=[SMEM, VMEM, VMEM],
        out_specs=[VMEM] * 2,
        compiler_params=params(16),
        name="both_weights",
    )(info, total, swap(total))


def finish_kernel(info, own_term, own, got, out):
    out[...] = (own_term[...] + whole_width(info[4], own[...], got[...])).astype(jnp.bfloat16)


def finish(info, own_term, own, got):
    return pl.pallas_call(
        finish_kernel,
        out_shape=jax.ShapeDtypeStruct(own_term.shape, jnp.bfloat16),
        in_specs=[SMEM] + [VMEM] * 3,
        out_specs=VMEM,
        compiler_params=params(16),
        name="finish",
    )(info, own_term, own, got)


def shards(features, w_self, w_neigh, cotangent, tile_values, tile_dst, tile_src, tile_count):
    row, col = lax.axis_index("row"), lax.axis_index("col")
    core = col % 2
    info = jnp.stack([row // 4, row % 4, col // 4, col // 2 % 2, core]).astype(jnp.int32)
    index = jnp.concatenate([tile_dst, tile_src, tile_count])
    first = core == 0
    mine = jnp.where(first, features[:, :256], features[:, 256:])
    theirs = jnp.where(first, features[:, 256:], features[:, :256])
    theirs = swap(theirs)
    theirs, tiles = lax.optimization_barrier((theirs, tile_values))
    work = ((index, tile_values), (swap(index), swap(tiles)))
    own, got, degree = aggregate(
        info, work, mine, theirs, degree_stages(info, index, tile_values), None
    )
    degree = jnp.broadcast_to(degree[0, 0][:, None], (degree.shape[-1], 128))
    output, grad_pre, mean, mine, theirs = dense(
        info, features, cotangent, w_self, w_neigh, degree, own, got
    )
    own, got, (total, own_term) = aggregate(
        info, work, mine, swap(theirs), weight_stages(info, features, w_self), (grad_pre, mean)
    )
    grad_self, grad_neigh = both_weights(info, total)
    grad_features = finish(info, own_term, own, got)
    return (output, grad_features, grad_self, grad_neigh)


def solution(mesh):
    return jax.shard_map(
        shards,
        mesh=mesh,
        in_specs=(
            P(("row", "col"), None),
            P(),
            P(),
            P(("row", "col"), None),
            P(("row", "col"), None, None),
            P(("row", "col")),
            P(("row", "col")),
            P(("row", "col")),
        ),
        out_specs=(P(("row", "col"), None), P(("row", "col"), None), P(), P()),
        check_vma=False,
    )
```

```python
import functools

import jax
import jax.numpy as jnp
from jax import lax
from jax.experimental import pallas as pl
from jax.experimental.pallas import tpu as pltpu
from jax.sharding import PartitionSpec as P

MIB = 1 << 20
UNROLL = 4
BOTH = ("row", "col")
CONTRACT_ROWS = (((0,), (0,)), ((), ()))
CONTRACT_COLS = (((1,), (1,)), ((), ()))

GATHER = (
    (("z", 1, 3), ("z", 3, 1), ("y", 1, 3), ("y", 3, 1)),
    (("y", 1, 3), ("y", 3, 1), ("z", 1, 3), ("z", 3, 1)),
)
ROWS = ((0, 176), (176, 80))
REDUCE = (
    (("x", 1, 3), ("x", 3, 1), ("l", 1, 1)),
    (("l", 1, 1), ("x", 1, 3), ("x", 3, 1)),
)
ROW_SUM = (("y", 1, 3), ("y", 3, 1), ("z", 1, 3), ("z", 3, 1))
AXES = ("y", "z", "x", "l", "c")
SIZES = (4, 4, 4, 2, 2)


def exchange(value, step):
    axis, *masks = step
    pairs = []
    for i in range(256):
        at, rest = {}, i
        for name, size in zip(reversed(AXES), reversed(SIZES)):
            at[name], rest = rest % size, rest // size
        at[axis] ^= masks[at["c"]]
        j = 0
        for name, size in zip(AXES, SIZES):
            j = j * size + at[name]
        pairs.append((i, j))
    return lax.ppermute(value, BOTH, pairs)


def swap(value):
    return exchange(value, ("c", 1, 1))


def place(info, steps, bits, core=None):
    at = {name: info[k] for k, name in enumerate(AXES)}
    core = info[4] if core is None else core
    for step, bit in zip(steps, bits):
        if bit:
            axis, first, second = step
            at[axis] = lax.bitwise_xor(at[axis], first + core * (second - first))
    return at


def params(limit):
    return pltpu.CompilerParams(vmem_limit_bytes=limit * MIB)


VMEM = pl.BlockSpec(memory_space=pltpu.VMEM)
SMEM = pl.BlockSpec(memory_space=pltpu.SMEM)
ANY = pl.BlockSpec(memory_space=pl.ANY)


def chip_slots(info, steps, core=None):
    chips = []
    for s in range(8):
        at = place(info, steps, (s >> 2 & 1, s >> 1 & 1, s & 1), core)
        chips.append(at["x"] * 2 + at["l"])
    return chips


def degree_kernel(info, index, tiles, own, other, acc):
    count, core = index[96], info[4]
    acc[...] = jnp.zeros_like(acc)

    def add(s):
        values = tiles[s].astype(jnp.float32)
        acc[index[s]] += values[:, :128] + values[:, 128:]

    def several(group, carry):
        for k in range(UNROLL):
            add(group * UNROLL + k)
        return carry

    def single(s, carry):
        add(s)
        return carry

    groups = lax.div(count, UNROLL)
    lax.fori_loop(0, groups, several, 0)
    lax.fori_loop(groups * UNROLL, count, single, 0)

    def sums(block):
        total = jnp.sum(jnp.transpose(acc[block]), axis=0, keepdims=True)
        return jnp.broadcast_to(total, (8, total.shape[1]))

    for s, chip in enumerate(chip_slots(info, REDUCE[0])):
        own[s] = sums(chip * 2 + core)
    for s, chip in enumerate(chip_slots(info, REDUCE[0], 1 - core)):
        other[s] = sums(chip * 2 + 1 - core)


def partial_degree(info, index, tiles):
    edge = tiles.shape[1]
    return pl.pallas_call(
        degree_kernel,
        out_shape=[jax.ShapeDtypeStruct((8, 8, edge), jnp.float32)] * 2,
        in_specs=[SMEM, SMEM, VMEM],
        out_specs=[VMEM] * 2,
        scratch_shapes=[
            pltpu.VMEM((16, edge, 128), jnp.float32),
        ],
        compiler_params=params(16),
        name="degree",
    )(info, index, tiles)


def degree_stages(info, index, tiles):
    def begin(state):
        own, other = partial_degree(info, index, tiles)
        return own + swap(other)

    def add(total, part):
        for step, n in part:
            total = total[:n] + exchange(total[n:], step)
        return total

    parts = list(zip(REDUCE[0], (4, 2, 1)))
    return {
        1: begin,
        2: lambda total: add(total, parts[:2]),
        3: lambda total: add(total, parts[2:]),
    }


def spread_kernel(info, index0, index1, tiles0, tiles1, *refs):
    pieces, (send0, keep0, send1, keep1, x, acc, buf, sem, piece_sem) = refs[:4], refs[4:]
    core = info[4]
    slots = tiles0.shape[0]

    copies = []
    for chain, (steps, (first, rows)) in enumerate(zip(GATHER, ROWS)):
        for s in range(16):
            at = place(info, steps, (s & 1, s >> 1 & 1, s >> 2 & 1, s >> 3))
            block = at["y"] * 4 + at["z"]
            copies.append(
                pltpu.make_async_copy(
                    pieces[chain * 2 + s // 8].at[s % 8],
                    x.at[pl.ds(block * 2, 2), pl.ds(first, rows), :],
                    piece_sem.at[chain, s],
                )
            )
    for copy in copies:
        copy.start()

    def tile_copy(tiles, base, s):
        return pltpu.make_async_copy(tiles.at[s], buf.at[base + s], sem.at[base + s])

    work = ((index0, tiles0, 0), (index1, tiles1, 1))
    for index, tiles, rel in work:

        def begin(s, carry, tiles=tiles, base=rel * slots):
            tile_copy(tiles, base, s).start()
            return carry

        lax.fori_loop(0, index[96], begin, 0)
    acc[...] = jnp.zeros_like(acc)
    for copy in copies:
        copy.wait()
    for index, tiles, rel in work:

        def multiply(s, index=index, rel=rel):
            acc[index[s]] += jnp.dot(
                buf[rel * slots + s],
                x[index[48 + s] * 2 + rel],
                preferred_element_type=jnp.float32,
            )

        def several(group, carry, tiles=tiles, rel=rel, multiply=multiply):
            for k in range(UNROLL):
                tile_copy(tiles, rel * slots, group * UNROLL + k).wait()
            for k in range(UNROLL):
                multiply(group * UNROLL + k)
            return carry

        def single(s, carry, tiles=tiles, rel=rel, multiply=multiply):
            tile_copy(tiles, rel * slots, s).wait()
            multiply(s)
            return carry

        groups = lax.div(index[96], UNROLL)
        lax.fori_loop(0, groups, several, 0)
        lax.fori_loop(groups * UNROLL, index[96], single, 0)
    for chain, (send, keep) in enumerate(((send0, keep0), (send1, keep1))):
        part = pl.ds(ROWS[chain][0], ROWS[chain][1])
        for s, chip in enumerate(chip_slots(info, REDUCE[chain])):
            for rel in range(2):
                block = chip * 2 + (core if rel == 0 else 1 - core)
                if s < 4:
                    keep[s, rel] = acc[block, part, :]
                else:
                    send[s - 4, rel] = acc[block, part, :].astype(jnp.bfloat16)


def spread(info, work, pieces):
    (index0, tiles0), (index1, tiles1) = work
    slots, edge, _ = tiles0.shape
    return pl.pallas_call(
        spread_kernel,
        out_shape=[
            jax.ShapeDtypeStruct((4, 2, rows, 256), dtype)
            for _, rows in ROWS
            for dtype in (jnp.bfloat16, jnp.float32)
        ],
        in_specs=[SMEM] * 3 + [ANY] * 6,
        out_specs=[VMEM] * 4,
        scratch_shapes=[
            pltpu.VMEM((32, edge, 256), jnp.bfloat16),
            pltpu.VMEM((16, edge, 256), jnp.float32),
            pltpu.VMEM((2 * slots, edge, edge), jnp.bfloat16),
            pltpu.SemaphoreType.DMA((2 * slots,)),
            pltpu.SemaphoreType.DMA((2, 16)),
        ],
        compiler_params=params(56),
        cost_estimate=pl.CostEstimate(
            flops=2 * 47 * edge * edge * 512, bytes_accessed=20 * MIB, transcendentals=0
        ),
        name="spread",
    )(info, index0, index1, tiles0, tiles1, *pieces)


def join_kernel(keep, got, send, rest):
    n = rest.shape[0]
    for s in range(2 * n):
        total = keep[s] + got[s].astype(jnp.float32)
        if s < n:
            rest[s] = total
        else:
            send[s - n] = total.astype(jnp.bfloat16)


def join(keep, got):
    shape = (keep.shape[0] // 2,) + keep.shape[1:]
    return pl.pallas_call(
        join_kernel,
        out_shape=[
            jax.ShapeDtypeStruct(shape, jnp.bfloat16),
            jax.ShapeDtypeStruct(shape, jnp.float32),
        ],
        in_specs=[VMEM] * 2,
        out_specs=[VMEM] * 2,
        compiler_params=params(16),
        name="join",
    )(keep, got)


def last_join_kernel(keep0, got0, keep1, got1, own, other):
    for chain, (keep, got) in enumerate(((keep0, got0), (keep1, got1))):
        part = pl.ds(ROWS[chain][0], ROWS[chain][1])
        own[part, :] = keep[0, 0] + got[0, 0].astype(jnp.float32)
        other[part, :] = keep[0, 1] + got[0, 1].astype(jnp.float32)


def last_join(keep0, got0, keep1, got1):
    edge = keep0.shape[2] + keep1.shape[2]
    return pl.pallas_call(
        last_join_kernel,
        out_shape=[jax.ShapeDtypeStruct((edge, 256), jnp.float32)] * 2,
        in_specs=[VMEM] * 4,
        out_specs=[VMEM] * 2,
        compiler_params=params(16),
        name="last_join",
    )(keep0, got0, keep1, got1)


def aggregate(info, work, own_half, arrived, stages, state):
    def beside(k, values, state):
        if k not in stages:
            return values, state
        return lax.optimization_barrier((values, stages[k](state)))

    pair = jnp.stack([own_half, arrived])
    have = [pair[None, :, first : first + rows] for first, rows in ROWS]
    for k in range(4):
        got = [exchange(h, steps[k]) for h, steps in zip(have, GATHER)]
        got, state = beside(k, got, state)
        if k < 3:
            have = [jnp.concatenate([h, g]) for h, g in zip(have, got)]
            have = lax.optimization_barrier(have)
    parts = spread(info, work, (have[0], got[0], have[1], got[1]))
    parts, state = beside(4, parts, state)
    send, keep = [parts[0], parts[2]], [parts[1], parts[3]]
    for k in range(2):
        arrived = [exchange(send[chain], REDUCE[chain][k]) for chain in range(2)]
        arrived = lax.optimization_barrier(arrived)
        arrived, state = beside(5 + k, arrived, state)
        for chain in range(2):
            send[chain], keep[chain] = join(keep[chain], arrived[chain])
        send, state = lax.optimization_barrier((send, state))
    arrived = [exchange(send[chain], REDUCE[chain][2]) for chain in range(2)]
    arrived, state = beside(7, arrived, state)
    own, other = last_join(keep[0], arrived[0], keep[1], arrived[1])
    return own, swap(other), state


def whole_width(core, own, got):
    first = core == 0
    return jnp.concatenate([jnp.where(first, own, got), jnp.where(first, got, own)], axis=1)


def dense_kernel(
    info, features, cotangent, w_self, w_neigh, degree, own, got, output, grad_pre, mean, mine, theirs
):
    deg = degree[:, 0:1]
    core = info[4]
    summed = whole_width(core, own[...], got[...])
    neighbor_mean = (summed / deg).astype(jnp.bfloat16)
    mean[...] = neighbor_mean
    preact = jnp.dot(features[...], w_self[...], preferred_element_type=jnp.float32) + jnp.dot(
        neighbor_mean, w_neigh[...], preferred_element_type=jnp.float32
    )
    part = jax.nn.sigmoid(preact)
    output[...] = (preact * part).astype(jnp.bfloat16)
    grad = (
        cotangent[...].astype(jnp.float32) * part * (1.0 + preact * (1.0 - part))
    ).astype(jnp.bfloat16)
    grad_pre[...] = grad
    back = (
        lax.dot_general(grad, w_neigh[...], CONTRACT_COLS, preferred_element_type=jnp.float32)
        / deg
    )
    mine[...] = jnp.where(core == 0, back[:, :256], back[:, 256:]).astype(jnp.bfloat16)
    theirs[...] = jnp.where(core == 0, back[:, 256:], back[:, :256]).astype(jnp.bfloat16)


def dense(info, features, cotangent, w_self, w_neigh, degree, own, got):
    nodes, width = features.shape
    full = jax.ShapeDtypeStruct((nodes, width), jnp.bfloat16)
    half = jax.ShapeDtypeStruct((nodes, 256), jnp.bfloat16)
    return pl.pallas_call(
        dense_kernel,
        out_shape=[full] * 3 + [half] * 2,
        in_specs=[SMEM] + [VMEM] * 7,
        out_specs=[VMEM] * 5,
        compiler_params=params(24),
        name="dense",
    )(info, features, cotangent, w_self, w_neigh, degree, own, got)


def weights_kernel(info, features, mean, grad_pre, w_self, keep, send, own):
    grad = grad_pre[...]
    grad_self = lax.dot_general(
        features[...], grad, CONTRACT_ROWS, preferred_element_type=jnp.float32
    )
    grad_neigh = lax.dot_general(
        mean[...], grad, CONTRACT_ROWS, preferred_element_type=jnp.float32
    )
    first = info[4] == 0
    keep[...] = jnp.where(first, grad_self, grad_neigh)
    send[...] = jnp.where(first, grad_neigh, grad_self)
    own[...] = lax.dot_general(
        grad, w_self[...], CONTRACT_COLS, preferred_element_type=jnp.float32
    )


def weights(info, features, mean, grad_pre, w_self):
    nodes, width = features.shape
    square = jax.ShapeDtypeStruct((width, width), jnp.float32)
    return pl.pallas_call(
        weights_kernel,
        out_shape=[square, square, jax.ShapeDtypeStruct((nodes, width), jnp.float32)],
        in_specs=[SMEM] + [VMEM] * 4,
        out_specs=[VMEM] * 3,
        compiler_params=params(24),
        name="weights",
    )(info, features, mean, grad_pre, w_self)


def weight_blocks_kernel(info, keep, got, send, rest):
    for s, chip in enumerate(chip_slots(info, REDUCE[0])):
        rows = pl.ds(pl.multiple_of(chip * 64, 64), 64)
        total = keep[rows, :] + got[rows, :]
        if s < 4:
            rest[s] = total
        else:
            send[s - 4] = total


def weight_blocks(info, keep, got):
    shape = jax.ShapeDtypeStruct((4, 64, keep.shape[1]), jnp.float32)
    return pl.pallas_call(
        weight_blocks_kernel,
        out_shape=[shape] * 2,
        in_specs=[SMEM, VMEM, VMEM],
        out_specs=[VMEM] * 2,
        compiler_params=params(16),
        name="weight_blocks",
    )(info, keep, got)


def weight_stages(info, features, w_self):
    steps = REDUCE[0]

    def local(state):
        grad_pre, mean = state
        keep, send, own_term = weights(info, features, mean, grad_pre, w_self)
        return keep, swap(send), own_term

    def first(state):
        keep, got, own_term = state
        send, rest = weight_blocks(info, keep, got)
        return rest + exchange(send, steps[0]), own_term

    def halve(step):
        def stage(state):
            total, own_term = state
            half = total.shape[0] // 2
            return total[:half] + exchange(total[half:], step), own_term

        return stage

    def row_sum(*chosen):
        def stage(state):
            total, own_term = state
            for step in chosen:
                total = total + exchange(total, step)
            return total, own_term

        return stage

    def collect(*chosen):
        def stage(state):
            total, own_term = state
            for step in chosen:
                total = jnp.concatenate([total, exchange(total, step)])
            return total, own_term

        return stage

    def others(total, axis):
        return [exchange(total, (axis, mask, mask)) for mask in (1, 2, 3)]

    def sum_y(state):
        total, own_term = state
        first, second, third = others(total, "y")
        return (total + first) + (second + third), own_term

    def collect_x(state):
        total, own_term = state
        return jnp.concatenate([total] + others(total, "x")), own_term

    sum_z, collect_l = row_sum(ROW_SUM[3]), collect(steps[2])
    return {
        0: local,
        1: first,
        2: halve(steps[1]),
        3: halve(steps[2]),
        4: sum_y,
        5: row_sum(ROW_SUM[2]),
        6: lambda state: collect_l(sum_z(state)),
        7: collect_x,
    }


def both_weights_kernel(info, mine, theirs, grad_self, grad_neigh):
    core = info[4]
    for value, owner in ((mine, core), (theirs, 1 - core)):
        for s in range(8):
            chip = lax.bitwise_xor(info[2], s // 2) * 2 + lax.bitwise_xor(info[3], s % 2)
            rows = pl.ds(pl.multiple_of(chip * 64, 64), 64)

            @pl.when(owner == 0)
            def _(value=value, s=s, rows=rows):
                grad_self[rows, :] = value[s]

            @pl.when(owner == 1)
            def _(value=value, s=s, rows=rows):
                grad_neigh[rows, :] = value[s]


def both_weights(info, total):
    width = total.shape[2]
    return pl.pallas_call(
        both_weights_kernel,
        out_shape=[jax.ShapeDtypeStruct((8 * total.shape[1], width), jnp.float32)] * 2,
        in_specs=[SMEM, VMEM, VMEM],
        out_specs=[VMEM] * 2,
        compiler_params=params(16),
        name="both_weights",
    )(info, total, swap(total))


def finish_kernel(info, own_term, own, got, out):
    out[...] = (own_term[...] + whole_width(info[4], own[...], got[...])).astype(jnp.bfloat16)


def finish(info, own_term, own, got):
    return pl.pallas_call(
        finish_kernel,
        out_shape=jax.ShapeDtypeStruct(own_term.shape, jnp.bfloat16),
        in_specs=[SMEM] + [VMEM] * 3,
        out_specs=VMEM,
        compiler_params=params(16),
        name="finish",
    )(info, own_term, own, got)


def shards(features, w_self, w_neigh, cotangent, tile_values, tile_dst, tile_src, tile_count):
    row, col = lax.axis_index("row"), lax.axis_index("col")
    core = col % 2
    info = jnp.stack([row // 4, row % 4, col // 4, col // 2 % 2, core]).astype(jnp.int32)
    index = jnp.concatenate([tile_dst, tile_src, tile_count])
    first = core == 0
    mine = jnp.where(first, features[:, :256], features[:, 256:])
    theirs = jnp.where(first, features[:, 256:], features[:, :256])
    theirs = swap(theirs)
    theirs, tiles = lax.optimization_barrier((theirs, tile_values))
    work = ((index, tile_values), (swap(index), swap(tiles)))
    own, got, degree = aggregate(
        info, work, mine, theirs, degree_stages(info, index, tile_values), None
    )
    degree = jnp.broadcast_to(degree[0, 0][:, None], (degree.shape[-1], 128))
    output, grad_pre, mean, mine, theirs = dense(
        info, features, cotangent, w_self, w_neigh, degree, own, got
    )
    own, got, (total, own_term) = aggregate(
        info, work, mine, swap(theirs), weight_stages(info, features, w_self), (grad_pre, mean)
    )
    grad_self, grad_neigh = both_weights(info, total)
    grad_features = finish(info, own_term, own, got)
    return (output, grad_features, grad_self, grad_neigh)


def solution(mesh):
    return jax.shard_map(
        shards,
        mesh=mesh,
        in_specs=(
            P(("row", "col"), None),
            P(),
            P(),
            P(("row", "col"), None),
            P(("row", "col"), None, None),
            P(("row", "col")),
            P(("row", "col")),
            P(("row", "col")),
        ),
        out_specs=(P(("row", "col"), None), P(("row", "col"), None), P(), P()),
        check_vma=False,
    )
```

```python
import functools

import jax
import jax.numpy as jnp
from jax import lax
from jax.experimental import pallas as pl
from jax.experimental.pallas import tpu as pltpu
from jax.sharding import PartitionSpec as P

MIB = 1 << 20
UNROLL = 4
BOTH = ("row", "col")
CONTRACT_ROWS = (((0,), (0,)), ((), ()))
CONTRACT_COLS = (((1,), (1,)), ((), ()))

GATHER = (
    (("z", 1, 3), ("z", 3, 1), ("y", 1, 3), ("y", 3, 1)),
    (("y", 1, 3), ("y", 3, 1), ("z", 1, 3), ("z", 3, 1)),
)
ROWS = ((0, 176), (176, 80))
REDUCE = (
    (("x", 1, 3), ("x", 3, 1), ("l", 1, 1)),
    (("l", 1, 1), ("x", 1, 3), ("x", 3, 1)),
)
ROW_SUM = (("y", 1, 3), ("y", 3, 1), ("z", 1, 3), ("z", 3, 1))
AXES = ("y", "z", "x", "l", "c")
SIZES = (4, 4, 4, 2, 2)


def exchange(value, step):
    axis, *masks = step
    pairs = []
    for i in range(256):
        at, rest = {}, i
        for name, size in zip(reversed(AXES), reversed(SIZES)):
            at[name], rest = rest % size, rest // size
        at[axis] ^= masks[at["c"]]
        j = 0
        for name, size in zip(AXES, SIZES):
            j = j * size + at[name]
        pairs.append((i, j))
    return lax.ppermute(value, BOTH, pairs)


def swap(value):
    return exchange(value, ("c", 1, 1))


def place(info, steps, bits, core=None):
    at = {name: info[k] for k, name in enumerate(AXES)}
    core = info[4] if core is None else core
    for step, bit in zip(steps, bits):
        if bit:
            axis, first, second = step
            at[axis] = lax.bitwise_xor(at[axis], first + core * (second - first))
    return at


def params(limit):
    return pltpu.CompilerParams(vmem_limit_bytes=limit * MIB)


VMEM = pl.BlockSpec(memory_space=pltpu.VMEM)
SMEM = pl.BlockSpec(memory_space=pltpu.SMEM)
ANY = pl.BlockSpec(memory_space=pl.ANY)


def chip_slots(info, steps, core=None):
    chips = []
    for s in range(8):
        at = place(info, steps, (s >> 2 & 1, s >> 1 & 1, s & 1), core)
        chips.append(at["x"] * 2 + at["l"])
    return chips


def degree_kernel(info, index, tiles, own, other, acc):
    count, core = index[96], info[4]
    acc[...] = jnp.zeros_like(acc)

    def add(s):
        values = tiles[s].astype(jnp.float32)
        acc[index[s]] += values[:, :128] + values[:, 128:]

    def several(group, carry):
        for k in range(UNROLL):
            add(group * UNROLL + k)
        return carry

    def single(s, carry):
        add(s)
        return carry

    groups = lax.div(count, UNROLL)
    lax.fori_loop(0, groups, several, 0)
    lax.fori_loop(groups * UNROLL, count, single, 0)

    def sums(block):
        total = jnp.sum(jnp.transpose(acc[block]), axis=0, keepdims=True)
        return jnp.broadcast_to(total, (8, total.shape[1]))

    for s, chip in enumerate(chip_slots(info, REDUCE[0])):
        own[s] = sums(chip * 2 + core)
    for s, chip in enumerate(chip_slots(info, REDUCE[0], 1 - core)):
        other[s] = sums(chip * 2 + 1 - core)


def partial_degree(info, index, tiles):
    edge = tiles.shape[1]
    return pl.pallas_call(
        degree_kernel,
        out_shape=[jax.ShapeDtypeStruct((8, 8, edge), jnp.float32)] * 2,
        in_specs=[SMEM, SMEM, VMEM],
        out_specs=[VMEM] * 2,
        scratch_shapes=[
            pltpu.VMEM((16, edge, 128), jnp.float32),
        ],
        compiler_params=params(16),
        name="degree",
    )(info, index, tiles)


def degree_stages(info, index, tiles):
    def begin(state):
        own, other = partial_degree(info, index, tiles)
        return own + swap(other)

    def add(total, part):
        for step, n in part:
            total = total[:n] + exchange(total[n:], step)
        return total

    parts = list(zip(REDUCE[0], (4, 2, 1)))
    return {
        1: begin,
        2: lambda total: add(total, parts[:2]),
        3: lambda total: add(total, parts[2:]),
    }


def spread_kernel(info, index0, index1, tiles0, tiles1, *refs):
    pieces, (send0, keep0, send1, keep1, x, acc, buf, sem, piece_sem) = refs[:4], refs[4:]
    core = info[4]
    slots = tiles0.shape[0]

    copies = []
    for chain, (steps, (first, rows)) in enumerate(zip(GATHER, ROWS)):
        for s in range(16):
            at = place(info, steps, (s & 1, s >> 1 & 1, s >> 2 & 1, s >> 3))
            block = at["y"] * 4 + at["z"]
            copies.append(
                pltpu.make_async_copy(
                    pieces[chain * 2 + s // 8].at[s % 8],
                    x.at[pl.ds(block * 2, 2), pl.ds(first, rows), :],
                    piece_sem.at[chain, s],
                )
            )
    for copy in copies:
        copy.start()

    def tile_copy(tiles, base, s):
        return pltpu.make_async_copy(tiles.at[s], buf.at[base + s], sem.at[base + s])

    first, second = index0[96], index1[96]

    def begin0(s, carry):
        tile_copy(tiles0, 0, s).start()
        return carry

    def begin1(s, carry):
        tile_copy(tiles1, slots, s).start()
        return carry

    lax.fori_loop(0, first, begin0, 0)
    lax.fori_loop(0, second, begin1, 0)

    def clear(block, carry):
        acc[block] = jnp.zeros(acc.shape[1:], acc.dtype)
        return carry

    lax.fori_loop(0, acc.shape[0], clear, 0)
    for copy in copies:
        copy.wait()

    def locate(t):
        rel = (t >= first).astype(jnp.int32)
        return t - rel * first, rel

    def arrive(t):
        s, rel = locate(t)
        tile_copy(tiles0, rel * slots, s).wait()

    def multiply(t):
        s, rel = locate(t)
        mine = rel == 0
        target = jnp.where(mine, index0[s], index1[s])
        source = jnp.where(mine, index0[48 + s], index1[48 + s])
        acc[target] += jnp.dot(
            buf[rel * slots + s], x[source * 2 + rel], preferred_element_type=jnp.float32
        )

    def several(group, carry):
        for k in range(UNROLL):
            arrive(group * UNROLL + k)
        for k in range(UNROLL):
            multiply(group * UNROLL + k)
        return carry

    def single(t, carry):
        arrive(t)
        multiply(t)
        return carry

    total = first + second
    groups = lax.div(total, UNROLL)
    lax.fori_loop(0, groups, several, 0)
    lax.fori_loop(groups * UNROLL, total, single, 0)
    for chain, (send, keep) in enumerate(((send0, keep0), (send1, keep1))):
        part = pl.ds(ROWS[chain][0], ROWS[chain][1])
        for s, chip in enumerate(chip_slots(info, REDUCE[chain])):
            for rel in range(2):
                block = chip * 2 + (core if rel == 0 else 1 - core)
                if s < 4:
                    keep[s, rel] = acc[block, part, :]
                else:
                    send[s - 4, rel] = acc[block, part, :].astype(jnp.bfloat16)


def spread(info, work, pieces):
    (index0, tiles0), (index1, tiles1) = work
    slots, edge, _ = tiles0.shape
    return pl.pallas_call(
        spread_kernel,
        out_shape=[
            jax.ShapeDtypeStruct((4, 2, rows, 256), dtype)
            for _, rows in ROWS
            for dtype in (jnp.bfloat16, jnp.float32)
        ],
        in_specs=[SMEM] * 3 + [ANY] * 6,
        out_specs=[VMEM] * 4,
        scratch_shapes=[
            pltpu.VMEM((32, edge, 256), jnp.bfloat16),
            pltpu.VMEM((16, edge, 256), jnp.float32),
            pltpu.VMEM((2 * slots, edge, edge), jnp.bfloat16),
            pltpu.SemaphoreType.DMA((2 * slots,)),
            pltpu.SemaphoreType.DMA((2, 16)),
        ],
        compiler_params=params(56),
        cost_estimate=pl.CostEstimate(
            flops=2 * 47 * edge * edge * 512, bytes_accessed=20 * MIB, transcendentals=0
        ),
        name="spread",
    )(info, index0, index1, tiles0, tiles1, *pieces)


def join_kernel(keep, got, send, rest):
    n = rest.shape[0]
    for s in range(2 * n):
        total = keep[s] + got[s].astype(jnp.float32)
        if s < n:
            rest[s] = total
        else:
            send[s - n] = total.astype(jnp.bfloat16)


def join(keep, got):
    shape = (keep.shape[0] // 2,) + keep.shape[1:]
    return pl.pallas_call(
        join_kernel,
        out_shape=[
            jax.ShapeDtypeStruct(shape, jnp.bfloat16),
            jax.ShapeDtypeStruct(shape, jnp.float32),
        ],
        in_specs=[VMEM] * 2,
        out_specs=[VMEM] * 2,
        compiler_params=params(16),
        name="join",
    )(keep, got)


def last_join_kernel(keep0, got0, keep1, got1, own, other):
    for chain, (keep, got) in enumerate(((keep0, got0), (keep1, got1))):
        part = pl.ds(ROWS[chain][0], ROWS[chain][1])
        own[part, :] = keep[0, 0] + got[0, 0].astype(jnp.float32)
        other[part, :] = keep[0, 1] + got[0, 1].astype(jnp.float32)


def last_join(keep0, got0, keep1, got1):
    edge = keep0.shape[2] + keep1.shape[2]
    return pl.pallas_call(
        last_join_kernel,
        out_shape=[jax.ShapeDtypeStruct((edge, 256), jnp.float32)] * 2,
        in_specs=[VMEM] * 4,
        out_specs=[VMEM] * 2,
        compiler_params=params(16),
        name="last_join",
    )(keep0, got0, keep1, got1)


def aggregate(info, work, own_half, arrived, stages, state):
    def beside(k, values, state):
        if k not in stages:
            return values, state
        return lax.optimization_barrier((values, stages[k](state)))

    pair = jnp.stack([own_half, arrived])
    have = [pair[None, :, first : first + rows] for first, rows in ROWS]
    for k in range(4):
        got = [exchange(h, steps[k]) for h, steps in zip(have, GATHER)]
        got, state = beside(k, got, state)
        if k < 3:
            have = [jnp.concatenate([h, g]) for h, g in zip(have, got)]
            have = lax.optimization_barrier(have)
    parts = spread(info, work, (have[0], got[0], have[1], got[1]))
    parts, state = beside(4, parts, state)
    send, keep = [parts[0], parts[2]], [parts[1], parts[3]]
    for k in range(2):
        arrived = [exchange(send[chain], REDUCE[chain][k]) for chain in range(2)]
        arrived = lax.optimization_barrier(arrived)
        arrived, state = beside(5 + k, arrived, state)
        for chain in range(2):
            send[chain], keep[chain] = join(keep[chain], arrived[chain])
        send, state = lax.optimization_barrier((send, state))
    arrived = [exchange(send[chain], REDUCE[chain][2]) for chain in range(2)]
    arrived, state = beside(7, arrived, state)
    own, other = last_join(keep[0], arrived[0], keep[1], arrived[1])
    return own, swap(other), state


def whole_width(core, own, got):
    first = core == 0
    return jnp.concatenate([jnp.where(first, own, got), jnp.where(first, got, own)], axis=1)


def dense_kernel(
    info, features, cotangent, w_self, w_neigh, degree, own, got, output, grad_pre, mean, mine, theirs
):
    deg = degree[:, 0:1]
    core = info[4]
    summed = whole_width(core, own[...], got[...])
    neighbor_mean = (summed / deg).astype(jnp.bfloat16)
    mean[...] = neighbor_mean
    preact = jnp.dot(features[...], w_self[...], preferred_element_type=jnp.float32) + jnp.dot(
        neighbor_mean, w_neigh[...], preferred_element_type=jnp.float32
    )
    part = jax.nn.sigmoid(preact)
    output[...] = (preact * part).astype(jnp.bfloat16)
    grad = (
        cotangent[...].astype(jnp.float32) * part * (1.0 + preact * (1.0 - part))
    ).astype(jnp.bfloat16)
    grad_pre[...] = grad
    back = (
        lax.dot_general(grad, w_neigh[...], CONTRACT_COLS, preferred_element_type=jnp.float32)
        / deg
    )
    mine[...] = jnp.where(core == 0, back[:, :256], back[:, 256:]).astype(jnp.bfloat16)
    theirs[...] = jnp.where(core == 0, back[:, 256:], back[:, :256]).astype(jnp.bfloat16)


def dense(info, features, cotangent, w_self, w_neigh, degree, own, got):
    nodes, width = features.shape
    full = jax.ShapeDtypeStruct((nodes, width), jnp.bfloat16)
    half = jax.ShapeDtypeStruct((nodes, 256), jnp.bfloat16)
    return pl.pallas_call(
        dense_kernel,
        out_shape=[full] * 3 + [half] * 2,
        in_specs=[SMEM] + [VMEM] * 7,
        out_specs=[VMEM] * 5,
        compiler_params=params(24),
        name="dense",
    )(info, features, cotangent, w_self, w_neigh, degree, own, got)


def weights_kernel(info, features, mean, grad_pre, w_self, keep, send, own):
    grad = grad_pre[...]
    grad_self = lax.dot_general(
        features[...], grad, CONTRACT_ROWS, preferred_element_type=jnp.float32
    )
    grad_neigh = lax.dot_general(
        mean[...], grad, CONTRACT_ROWS, preferred_element_type=jnp.float32
    )
    first = info[4] == 0
    keep[...] = jnp.where(first, grad_self, grad_neigh)
    send[...] = jnp.where(first, grad_neigh, grad_self)
    own[...] = lax.dot_general(
        grad, w_self[...], CONTRACT_COLS, preferred_element_type=jnp.float32
    )


def weights(info, features, mean, grad_pre, w_self):
    nodes, width = features.shape
    square = jax.ShapeDtypeStruct((width, width), jnp.float32)
    return pl.pallas_call(
        weights_kernel,
        out_shape=[square, square, jax.ShapeDtypeStruct((nodes, width), jnp.float32)],
        in_specs=[SMEM] + [VMEM] * 4,
        out_specs=[VMEM] * 3,
        compiler_params=params(24),
        name="weights",
    )(info, features, mean, grad_pre, w_self)


def weight_blocks_kernel(info, keep, got, send, rest):
    for s, chip in enumerate(chip_slots(info, REDUCE[0])):
        rows = pl.ds(pl.multiple_of(chip * 64, 64), 64)
        total = keep[rows, :] + got[rows, :]
        if s < 4:
            rest[s] = total
        else:
            send[s - 4] = total


def weight_blocks(info, keep, got):
    shape = jax.ShapeDtypeStruct((4, 64, keep.shape[1]), jnp.float32)
    return pl.pallas_call(
        weight_blocks_kernel,
        out_shape=[shape] * 2,
        in_specs=[SMEM, VMEM, VMEM],
        out_specs=[VMEM] * 2,
        compiler_params=params(16),
        name="weight_blocks",
    )(info, keep, got)


def weight_stages(info, features, w_self):
    steps = REDUCE[0]

    def local(state):
        grad_pre, mean = state
        keep, send, own_term = weights(info, features, mean, grad_pre, w_self)
        return keep, swap(send), own_term

    def first(state):
        keep, got, own_term = state
        send, rest = weight_blocks(info, keep, got)
        return rest + exchange(send, steps[0]), own_term

    def halve(step):
        def stage(state):
            total, own_term = state
            half = total.shape[0] // 2
            return total[:half] + exchange(total[half:], step), own_term

        return stage

    def row_sum(*chosen):
        def stage(state):
            total, own_term = state
            for step in chosen:
                total = total + exchange(total, step)
            return total, own_term

        return stage

    def collect(*chosen):
        def stage(state):
            total, own_term = state
            for step in chosen:
                total = jnp.concatenate([total, exchange(total, step)])
            return total, own_term

        return stage

    def others(total, axis):
        return [exchange(total, (axis, mask, mask)) for mask in (1, 2, 3)]

    def sum_y(state):
        total, own_term = state
        first, second, third = others(total, "y")
        return (total + first) + (second + third), own_term

    def collect_x(state):
        total, own_term = state
        return jnp.concatenate([total] + others(total, "x")), own_term

    sum_z, collect_l = row_sum(ROW_SUM[3]), collect(steps[2])
    return {
        0: local,
        1: first,
        2: halve(steps[1]),
        3: halve(steps[2]),
        4: sum_y,
        5: row_sum(ROW_SUM[2]),
        6: lambda state: collect_l(sum_z(state)),
        7: collect_x,
    }


def both_weights_kernel(info, mine, theirs, grad_self, grad_neigh):
    core = info[4]
    for value, owner in ((mine, core), (theirs, 1 - core)):
        for s in range(8):
            chip = lax.bitwise_xor(info[2], s // 2) * 2 + lax.bitwise_xor(info[3], s % 2)
            rows = pl.ds(pl.multiple_of(chip * 64, 64), 64)

            @pl.when(owner == 0)
            def _(value=value, s=s, rows=rows):
                grad_self[rows, :] = value[s]

            @pl.when(owner == 1)
            def _(value=value, s=s, rows=rows):
                grad_neigh[rows, :] = value[s]


def both_weights(info, total):
    width = total.shape[2]
    return pl.pallas_call(
        both_weights_kernel,
        out_shape=[jax.ShapeDtypeStruct((8 * total.shape[1], width), jnp.float32)] * 2,
        in_specs=[SMEM, VMEM, VMEM],
        out_specs=[VMEM] * 2,
        compiler_params=params(16),
        name="both_weights",
    )(info, total, swap(total))


def finish_kernel(info, own_term, own, got, out):
    out[...] = (own_term[...] + whole_width(info[4], own[...], got[...])).astype(jnp.bfloat16)


def finish(info, own_term, own, got):
    return pl.pallas_call(
        finish_kernel,
        out_shape=jax.ShapeDtypeStruct(own_term.shape, jnp.bfloat16),
        in_specs=[SMEM] + [VMEM] * 3,
        out_specs=VMEM,
        compiler_params=params(16),
        name="finish",
    )(info, own_term, own, got)


def shards(features, w_self, w_neigh, cotangent, tile_values, tile_dst, tile_src, tile_count):
    row, col = lax.axis_index("row"), lax.axis_index("col")
    core = col % 2
    info = jnp.stack([row // 4, row % 4, col // 4, col // 2 % 2, core]).astype(jnp.int32)
    index = jnp.concatenate([tile_dst, tile_src, tile_count])
    first = core == 0
    mine = jnp.where(first, features[:, :256], features[:, 256:])
    theirs = jnp.where(first, features[:, 256:], features[:, :256])
    theirs = swap(theirs)
    theirs, tiles = lax.optimization_barrier((theirs, tile_values))
    work = ((index, tile_values), (swap(index), swap(tiles)))
    own, got, degree = aggregate(
        info, work, mine, theirs, degree_stages(info, index, tile_values), None
    )
    degree = jnp.broadcast_to(degree[0, 0][:, None], (degree.shape[-1], 128))
    output, grad_pre, mean, mine, theirs = dense(
        info, features, cotangent, w_self, w_neigh, degree, own, got
    )
    own, got, (total, own_term) = aggregate(
        info, work, mine, swap(theirs), weight_stages(info, features, w_self), (grad_pre, mean)
    )
    grad_self, grad_neigh = both_weights(info, total)
    grad_features = finish(info, own_term, own, got)
    return (output, grad_features, grad_self, grad_neigh)


def solution(mesh):
    return jax.shard_map(
        shards,
        mesh=mesh,
        in_specs=(
            P(("row", "col"), None),
            P(),
            P(),
            P(("row", "col"), None),
            P(("row", "col"), None, None),
            P(("row", "col")),
            P(("row", "col")),
            P(("row", "col")),
        ),
        out_specs=(P(("row", "col"), None), P(("row", "col"), None), P(), P()),
        check_vma=False,
    )
```

```python
import functools

import jax
import jax.numpy as jnp
from jax import lax
from jax.experimental import pallas as pl
from jax.experimental.pallas import tpu as pltpu
from jax.sharding import PartitionSpec as P

MIB = 1 << 20
UNROLL = 4
BOTH = ("row", "col")
CONTRACT_ROWS = (((0,), (0,)), ((), ()))
CONTRACT_COLS = (((1,), (1,)), ((), ()))

GATHER = (
    (("z", 1, 3), ("z", 3, 1), ("y", 1, 3), ("y", 3, 1)),
    (("y", 1, 3), ("y", 3, 1), ("z", 1, 3), ("z", 3, 1)),
)
ROWS = ((0, 176), (176, 80))
REDUCE = (
    (("x", 1, 3), ("x", 3, 1), ("l", 1, 1)),
    (("l", 1, 1), ("x", 1, 3), ("x", 3, 1)),
)
ROW_SUM = (("y", 1, 3), ("y", 3, 1), ("z", 1, 3), ("z", 3, 1))
AXES = ("y", "z", "x", "l", "c")
SIZES = (4, 4, 4, 2, 2)


def exchange(value, step):
    axis, *masks = step
    pairs = []
    for i in range(256):
        at, rest = {}, i
        for name, size in zip(reversed(AXES), reversed(SIZES)):
            at[name], rest = rest % size, rest // size
        at[axis] ^= masks[at["c"]]
        j = 0
        for name, size in zip(AXES, SIZES):
            j = j * size + at[name]
        pairs.append((i, j))
    return lax.ppermute(value, BOTH, pairs)


def swap(value):
    return exchange(value, ("c", 1, 1))


def place(info, steps, bits, core=None):
    at = {name: info[k] for k, name in enumerate(AXES)}
    core = info[4] if core is None else core
    for step, bit in zip(steps, bits):
        if bit:
            axis, first, second = step
            at[axis] = lax.bitwise_xor(at[axis], first + core * (second - first))
    return at


def params(limit):
    return pltpu.CompilerParams(vmem_limit_bytes=limit * MIB)


VMEM = pl.BlockSpec(memory_space=pltpu.VMEM)
SMEM = pl.BlockSpec(memory_space=pltpu.SMEM)
ANY = pl.BlockSpec(memory_space=pl.ANY)


def chip_slots(info, steps, core=None):
    chips = []
    for s in range(8):
        at = place(info, steps, (s >> 2 & 1, s >> 1 & 1, s & 1), core)
        chips.append(at["x"] * 2 + at["l"])
    return chips


def degree_kernel(info, index, tiles, own, other, acc):
    count, core = index[96], info[4]
    acc[...] = jnp.zeros_like(acc)

    def add(s):
        values = tiles[s].astype(jnp.float32)
        acc[index[s]] += values[:, :128] + values[:, 128:]

    def several(group, carry):
        for k in range(UNROLL):
            add(group * UNROLL + k)
        return carry

    def single(s, carry):
        add(s)
        return carry

    groups = lax.div(count, UNROLL)
    lax.fori_loop(0, groups, several, 0)
    lax.fori_loop(groups * UNROLL, count, single, 0)

    def sums(block):
        total = jnp.sum(jnp.transpose(acc[block]), axis=0, keepdims=True)
        return jnp.broadcast_to(total, (8, total.shape[1]))

    for s, chip in enumerate(chip_slots(info, REDUCE[0])):
        own[s] = sums(chip * 2 + core)
    for s, chip in enumerate(chip_slots(info, REDUCE[0], 1 - core)):
        other[s] = sums(chip * 2 + 1 - core)


def partial_degree(info, index, tiles):
    edge = tiles.shape[1]
    return pl.pallas_call(
        degree_kernel,
        out_shape=[jax.ShapeDtypeStruct((8, 8, edge), jnp.float32)] * 2,
        in_specs=[SMEM, SMEM, VMEM],
        out_specs=[VMEM] * 2,
        scratch_shapes=[
            pltpu.VMEM((16, edge, 128), jnp.float32),
        ],
        compiler_params=params(16),
        name="degree",
    )(info, index, tiles)


def degree_stages(info, index, tiles):
    def begin(state):
        own, other = partial_degree(info, index, tiles)
        return own + swap(other)

    def add(total, part):
        for step, n in part:
            total = total[:n] + exchange(total[n:], step)
        return total

    parts = list(zip(REDUCE[0], (4, 2, 1)))
    return {
        1: begin,
        2: lambda total: add(total, parts[:2]),
        3: lambda total: add(total, parts[2:]),
    }


def spread_kernel(info, index0, index1, tiles0, tiles1, *refs):
    pieces, (send0, keep0, send1, keep1, x, acc, buf, sem, piece_sem) = refs[:4], refs[4:]
    core = info[4]
    slots = tiles0.shape[0]

    copies = []
    for chain, (steps, (first, rows)) in enumerate(zip(GATHER, ROWS)):
        for s in range(16):
            at = place(info, steps, (s & 1, s >> 1 & 1, s >> 2 & 1, s >> 3))
            block = at["y"] * 4 + at["z"]
            copies.append(
                pltpu.make_async_copy(
                    pieces[chain * 2 + s // 8].at[s % 8],
                    x.at[pl.ds(block * 2, 2), pl.ds(first, rows), :],
                    piece_sem.at[chain, s],
                )
            )
    for copy in copies:
        copy.start()

    def tile_copy(tiles, base, s):
        return pltpu.make_async_copy(tiles.at[s], buf.at[base + s], sem.at[base + s])

    first, second = index0[96], index1[96]

    def begin0(s, carry):
        tile_copy(tiles0, 0, s).start()
        return carry

    def begin1(s, carry):
        tile_copy(tiles1, slots, s).start()
        return carry

    lax.fori_loop(0, first, begin0, 0)
    lax.fori_loop(0, second, begin1, 0)

    def clear(block, carry):
        acc[block] = jnp.zeros(acc.shape[1:], acc.dtype)
        return carry

    lax.fori_loop(0, acc.shape[0], clear, 0)
    for copy in copies:
        copy.wait()

    def locate(t):
        rel = (t >= first).astype(jnp.int32)
        return t - rel * first, rel

    def arrive(t):
        s, rel = locate(t)
        tile_copy(tiles0, rel * slots, s).wait()

    def multiply(t):
        s, rel = locate(t)
        mine = rel == 0
        target = jnp.where(mine, index0[s], index1[s])
        source = jnp.where(mine, index0[48 + s], index1[48 + s])
        acc[target] += jnp.dot(
            buf[rel * slots + s], x[source * 2 + rel], preferred_element_type=jnp.float32
        )

    def several(group, carry):
        for k in range(UNROLL):
            arrive(group * UNROLL + k)
        for k in range(UNROLL):
            multiply(group * UNROLL + k)
        return carry

    def single(t, carry):
        arrive(t)
        multiply(t)
        return carry

    total = first + second
    groups = lax.div(total, UNROLL)
    lax.fori_loop(0, groups, several, 0)
    lax.fori_loop(groups * UNROLL, total, single, 0)
    for chain, (send, keep) in enumerate(((send0, keep0), (send1, keep1))):
        part = pl.ds(ROWS[chain][0], ROWS[chain][1])
        for s, chip in enumerate(chip_slots(info, REDUCE[chain])):
            for rel in range(2):
                block = chip * 2 + (core if rel == 0 else 1 - core)
                if s < 4:
                    keep[s, rel] = acc[block, part, :]
                else:
                    send[s - 4, rel] = acc[block, part, :].astype(jnp.bfloat16)


def spread(info, work, pieces):
    (index0, tiles0), (index1, tiles1) = work
    slots, edge, _ = tiles0.shape
    return pl.pallas_call(
        spread_kernel,
        out_shape=[
            jax.ShapeDtypeStruct((4, 2, rows, 256), dtype)
            for _, rows in ROWS
            for dtype in (jnp.bfloat16, jnp.float32)
        ],
        in_specs=[SMEM] * 3 + [ANY] * 6,
        out_specs=[VMEM] * 4,
        scratch_shapes=[
            pltpu.VMEM((32, edge, 256), jnp.bfloat16),
            pltpu.VMEM((16, edge, 256), jnp.float32),
            pltpu.VMEM((2 * slots, edge, edge), jnp.bfloat16),
            pltpu.SemaphoreType.DMA((2 * slots,)),
            pltpu.SemaphoreType.DMA((2, 16)),
        ],
        compiler_params=params(56),
        cost_estimate=pl.CostEstimate(
            flops=2 * 47 * edge * edge * 512, bytes_accessed=20 * MIB, transcendentals=0
        ),
        name="spread",
    )(info, index0, index1, tiles0, tiles1, *pieces)


def join_kernel(keep, got, send, rest):
    n = rest.shape[0]
    for s in range(2 * n):
        total = keep[s] + got[s].astype(jnp.float32)
        if s < n:
            rest[s] = total
        else:
            send[s - n] = total.astype(jnp.bfloat16)


def join(keep, got):
    shape = (keep.shape[0] // 2,) + keep.shape[1:]
    return pl.pallas_call(
        join_kernel,
        out_shape=[
            jax.ShapeDtypeStruct(shape, jnp.bfloat16),
            jax.ShapeDtypeStruct(shape, jnp.float32),
        ],
        in_specs=[VMEM] * 2,
        out_specs=[VMEM] * 2,
        compiler_params=params(16),
        name="join",
    )(keep, got)


def last_join_kernel(keep0, got0, keep1, got1, own, other):
    for chain, (keep, got) in enumerate(((keep0, got0), (keep1, got1))):
        part = pl.ds(ROWS[chain][0], ROWS[chain][1])
        own[part, :] = keep[0, 0] + got[0, 0].astype(jnp.float32)
        other[part, :] = keep[0, 1] + got[0, 1].astype(jnp.float32)


def last_join(keep0, got0, keep1, got1):
    edge = keep0.shape[2] + keep1.shape[2]
    return pl.pallas_call(
        last_join_kernel,
        out_shape=[jax.ShapeDtypeStruct((edge, 256), jnp.float32)] * 2,
        in_specs=[VMEM] * 4,
        out_specs=[VMEM] * 2,
        compiler_params=params(16),
        name="last_join",
    )(keep0, got0, keep1, got1)


def aggregate(info, work, own_half, arrived, stages, state):
    def beside(k, values, state):
        if k not in stages:
            return values, state
        return lax.optimization_barrier((values, stages[k](state)))

    pair = jnp.stack([own_half, arrived])
    have = [pair[None, :, first : first + rows] for first, rows in ROWS]
    for k in range(4):
        got = [exchange(h, steps[k]) for h, steps in zip(have, GATHER)]
        got, state = beside(k, got, state)
        if k < 3:
            have = [jnp.concatenate([h, g]) for h, g in zip(have, got)]
            have = lax.optimization_barrier(have)
    parts = spread(info, work, (have[0], got[0], have[1], got[1]))
    parts, state = beside(4, parts, state)
    send, keep = [parts[0], parts[2]], [parts[1], parts[3]]
    for k in range(2):
        arrived = [exchange(send[chain], REDUCE[chain][k]) for chain in range(2)]
        if 5 + k in stages:
            state = stages[5 + k](state)
        if k == 1 and "after" in stages:
            state, arrived[1] = lax.optimization_barrier((state, arrived[1]))
            state = stages["after"](state)
        arrived, state = lax.optimization_barrier((arrived, state))
        for chain in range(2):
            send[chain], keep[chain] = join(keep[chain], arrived[chain])
        send, state = lax.optimization_barrier((send, state))
    arrived = [exchange(send[chain], REDUCE[chain][2]) for chain in range(2)]
    arrived, state = beside(7, arrived, state)
    own, other = last_join(keep[0], arrived[0], keep[1], arrived[1])
    return own, swap(other), state


def whole_width(core, own, got):
    first = core == 0
    return jnp.concatenate([jnp.where(first, own, got), jnp.where(first, got, own)], axis=1)


def dense_kernel(
    info, features, cotangent, w_self, w_neigh, degree, own, got, output, grad_pre, mean, mine, theirs
):
    deg = degree[:, 0:1]
    core = info[4]
    summed = whole_width(core, own[...], got[...])
    neighbor_mean = (summed / deg).astype(jnp.bfloat16)
    mean[...] = neighbor_mean
    preact = jnp.dot(features[...], w_self[...], preferred_element_type=jnp.float32) + jnp.dot(
        neighbor_mean, w_neigh[...], preferred_element_type=jnp.float32
    )
    part = jax.nn.sigmoid(preact)
    output[...] = (preact * part).astype(jnp.bfloat16)
    grad = (
        cotangent[...].astype(jnp.float32) * part * (1.0 + preact * (1.0 - part))
    ).astype(jnp.bfloat16)
    grad_pre[...] = grad
    back = (
        lax.dot_general(grad, w_neigh[...], CONTRACT_COLS, preferred_element_type=jnp.float32)
        / deg
    )
    mine[...] = jnp.where(core == 0, back[:, :256], back[:, 256:]).astype(jnp.bfloat16)
    theirs[...] = jnp.where(core == 0, back[:, 256:], back[:, :256]).astype(jnp.bfloat16)


def dense(info, features, cotangent, w_self, w_neigh, degree, own, got):
    nodes, width = features.shape
    full = jax.ShapeDtypeStruct((nodes, width), jnp.bfloat16)
    half = jax.ShapeDtypeStruct((nodes, 256), jnp.bfloat16)
    return pl.pallas_call(
        dense_kernel,
        out_shape=[full] * 3 + [half] * 2,
        in_specs=[SMEM] + [VMEM] * 7,
        out_specs=[VMEM] * 5,
        compiler_params=params(24),
        name="dense",
    )(info, features, cotangent, w_self, w_neigh, degree, own, got)


def weights_kernel(info, features, mean, grad_pre, w_self, keep, send, own):
    grad = grad_pre[...]
    grad_self = lax.dot_general(
        features[...], grad, CONTRACT_ROWS, preferred_element_type=jnp.float32
    )
    grad_neigh = lax.dot_general(
        mean[...], grad, CONTRACT_ROWS, preferred_element_type=jnp.float32
    )
    first = info[4] == 0
    keep[...] = jnp.where(first, grad_self, grad_neigh)
    send[...] = jnp.where(first, grad_neigh, grad_self)
    own[...] = lax.dot_general(
        grad, w_self[...], CONTRACT_COLS, preferred_element_type=jnp.float32
    )


def weights(info, features, mean, grad_pre, w_self):
    nodes, width = features.shape
    square = jax.ShapeDtypeStruct((width, width), jnp.float32)
    return pl.pallas_call(
        weights_kernel,
        out_shape=[square, square, jax.ShapeDtypeStruct((nodes, width), jnp.float32)],
        in_specs=[SMEM] + [VMEM] * 4,
        out_specs=[VMEM] * 3,
        compiler_params=params(24),
        name="weights",
    )(info, features, mean, grad_pre, w_self)


def weight_blocks_kernel(info, keep, got, send, rest):
    for s, chip in enumerate(chip_slots(info, REDUCE[0])):
        rows = pl.ds(pl.multiple_of(chip * 64, 64), 64)
        total = keep[rows, :] + got[rows, :]
        if s < 4:
            rest[s] = total
        else:
            send[s - 4] = total


def weight_blocks(info, keep, got):
    shape = jax.ShapeDtypeStruct((4, 64, keep.shape[1]), jnp.float32)
    return pl.pallas_call(
        weight_blocks_kernel,
        out_shape=[shape] * 2,
        in_specs=[SMEM, VMEM, VMEM],
        out_specs=[VMEM] * 2,
        compiler_params=params(16),
        name="weight_blocks",
    )(info, keep, got)


def weight_stages(info, features, w_self):
    steps = REDUCE[0]

    def local(state):
        grad_pre, mean = state
        keep, send, own_term = weights(info, features, mean, grad_pre, w_self)
        return keep, swap(send), own_term

    def first(state):
        keep, got, own_term = state
        send, rest = weight_blocks(info, keep, got)
        return rest + exchange(send, steps[0]), own_term

    def halve(step):
        def stage(state):
            total, own_term = state
            half = total.shape[0] // 2
            return total[:half] + exchange(total[half:], step), own_term

        return stage

    def row_sum(*chosen):
        def stage(state):
            total, own_term = state
            for step in chosen:
                total = total + exchange(total, step)
            return total, own_term

        return stage

    def collect(*chosen):
        def stage(state):
            total, own_term = state
            for step in chosen:
                total = jnp.concatenate([total, exchange(total, step)])
            return total, own_term

        return stage

    def others(total, axis):
        return [exchange(total, (axis, mask, mask)) for mask in (1, 2, 3)]

    def sum_y(state):
        total, own_term = state
        first, second, third = others(total, "y")
        return (total + first) + (second + third), own_term

    def collect_x(state):
        total, own_term = state
        return jnp.concatenate([total] + others(total, "x")), own_term

    return {
        0: local,
        1: first,
        2: halve(steps[1]),
        3: halve(steps[2]),
        4: sum_y,
        5: row_sum(ROW_SUM[2]),
        6: row_sum(ROW_SUM[3]),
        "after": collect(steps[2]),
        7: collect_x,
    }


def both_weights_kernel(info, mine, theirs, grad_self, grad_neigh):
    core = info[4]
    for value, owner in ((mine, core), (theirs, 1 - core)):
        for s in range(8):
            chip = lax.bitwise_xor(info[2], s // 2) * 2 + lax.bitwise_xor(info[3], s % 2)
            rows = pl.ds(pl.multiple_of(chip * 64, 64), 64)

            @pl.when(owner == 0)
            def _(value=value, s=s, rows=rows):
                grad_self[rows, :] = value[s]

            @pl.when(owner == 1)
            def _(value=value, s=s, rows=rows):
                grad_neigh[rows, :] = value[s]


def both_weights(info, total):
    width = total.shape[2]
    return pl.pallas_call(
        both_weights_kernel,
        out_shape=[jax.ShapeDtypeStruct((8 * total.shape[1], width), jnp.float32)] * 2,
        in_specs=[SMEM, VMEM, VMEM],
        out_specs=[VMEM] * 2,
        compiler_params=params(16),
        name="both_weights",
    )(info, total, swap(total))


def finish_kernel(info, own_term, own, got, out):
    out[...] = (own_term[...] + whole_width(info[4], own[...], got[...])).astype(jnp.bfloat16)


def finish(info, own_term, own, got):
    return pl.pallas_call(
        finish_kernel,
        out_shape=jax.ShapeDtypeStruct(own_term.shape, jnp.bfloat16),
        in_specs=[SMEM] + [VMEM] * 3,
        out_specs=VMEM,
        compiler_params=params(16),
        name="finish",
    )(info, own_term, own, got)


def shards(features, w_self, w_neigh, cotangent, tile_values, tile_dst, tile_src, tile_count):
    row, col = lax.axis_index("row"), lax.axis_index("col")
    core = col % 2
    info = jnp.stack([row // 4, row % 4, col // 4, col // 2 % 2, core]).astype(jnp.int32)
    index = jnp.concatenate([tile_dst, tile_src, tile_count])
    first = core == 0
    mine = jnp.where(first, features[:, :256], features[:, 256:])
    theirs = jnp.where(first, features[:, 256:], features[:, :256])
    theirs = swap(theirs)
    theirs, tiles = lax.optimization_barrier((theirs, tile_values))
    work = ((index, tile_values), (swap(index), swap(tiles)))
    own, got, degree = aggregate(
        info, work, mine, theirs, degree_stages(info, index, tile_values), None
    )
    degree = jnp.broadcast_to(degree[0, 0][:, None], (degree.shape[-1], 128))
    output, grad_pre, mean, mine, theirs = dense(
        info, features, cotangent, w_self, w_neigh, degree, own, got
    )
    own, got, (total, own_term) = aggregate(
        info, work, mine, swap(theirs), weight_stages(info, features, w_self), (grad_pre, mean)
    )
    grad_self, grad_neigh = both_weights(info, total)
    grad_features = finish(info, own_term, own, got)
    return (output, grad_features, grad_self, grad_neigh)


def solution(mesh):
    return jax.shard_map(
        shards,
        mesh=mesh,
        in_specs=(
            P(("row", "col"), None),
            P(),
            P(),
            P(("row", "col"), None),
            P(("row", "col"), None, None),
            P(("row", "col")),
            P(("row", "col")),
            P(("row", "col")),
        ),
        out_specs=(P(("row", "col"), None), P(("row", "col"), None), P(), P()),
        check_vma=False,
    )
```

```python
import functools

import jax
import jax.numpy as jnp
from jax import lax
from jax.experimental import pallas as pl
from jax.experimental.pallas import tpu as pltpu
from jax.sharding import PartitionSpec as P

MIB = 1 << 20
UNROLL = 4
BOTH = ("row", "col")
CONTRACT_ROWS = (((0,), (0,)), ((), ()))
CONTRACT_COLS = (((1,), (1,)), ((), ()))

GATHER = (
    (("z", 1, 3), ("z", 3, 1), ("y", 1, 3), ("y", 3, 1)),
    (("y", 1, 3), ("y", 3, 1), ("z", 1, 3), ("z", 3, 1)),
)
ROWS = ((0, 176), (176, 80))
REDUCE = (
    (("x", 1, 3), ("x", 3, 1), ("l", 1, 1)),
    (("l", 1, 1), ("x", 1, 3), ("x", 3, 1)),
)
ROW_SUM = (("y", 1, 3), ("y", 3, 1), ("z", 1, 3), ("z", 3, 1))
AXES = ("y", "z", "x", "l", "c")
SIZES = (4, 4, 4, 2, 2)


def exchange(value, step):
    axis, *masks = step
    pairs = []
    for i in range(256):
        at, rest = {}, i
        for name, size in zip(reversed(AXES), reversed(SIZES)):
            at[name], rest = rest % size, rest // size
        at[axis] ^= masks[at["c"]]
        j = 0
        for name, size in zip(AXES, SIZES):
            j = j * size + at[name]
        pairs.append((i, j))
    return lax.ppermute(value, BOTH, pairs)


def swap(value):
    return exchange(value, ("c", 1, 1))


def place(info, steps, bits, core=None):
    at = {name: info[k] for k, name in enumerate(AXES)}
    core = info[4] if core is None else core
    for step, bit in zip(steps, bits):
        if bit:
            axis, first, second = step
            at[axis] = lax.bitwise_xor(at[axis], first + core * (second - first))
    return at


def params(limit):
    return pltpu.CompilerParams(vmem_limit_bytes=limit * MIB)


VMEM = pl.BlockSpec(memory_space=pltpu.VMEM)
SMEM = pl.BlockSpec(memory_space=pltpu.SMEM)
ANY = pl.BlockSpec(memory_space=pl.ANY)


def chip_slots(info, steps, core=None):
    chips = []
    for s in range(8):
        at = place(info, steps, (s >> 2 & 1, s >> 1 & 1, s & 1), core)
        chips.append(at["x"] * 2 + at["l"])
    return chips


def degree_kernel(info, index, tiles, own, other, acc):
    count, core = index[96], info[4]
    acc[...] = jnp.zeros_like(acc)

    def add(s):
        values = tiles[s].astype(jnp.float32)
        acc[index[s]] += values[:, :128] + values[:, 128:]

    def several(group, carry):
        for k in range(UNROLL):
            add(group * UNROLL + k)
        return carry

    def single(s, carry):
        add(s)
        return carry

    groups = lax.div(count, UNROLL)
    lax.fori_loop(0, groups, several, 0)
    lax.fori_loop(groups * UNROLL, count, single, 0)

    def sums(block):
        total = jnp.sum(jnp.transpose(acc[block]), axis=0, keepdims=True)
        return jnp.broadcast_to(total, (8, total.shape[1]))

    for s, chip in enumerate(chip_slots(info, REDUCE[0])):
        own[s] = sums(chip * 2 + core)
    for s, chip in enumerate(chip_slots(info, REDUCE[0], 1 - core)):
        other[s] = sums(chip * 2 + 1 - core)


def partial_degree(info, index, tiles):
    edge = tiles.shape[1]
    return pl.pallas_call(
        degree_kernel,
        out_shape=[jax.ShapeDtypeStruct((8, 8, edge), jnp.float32)] * 2,
        in_specs=[SMEM, SMEM, VMEM],
        out_specs=[VMEM] * 2,
        scratch_shapes=[
            pltpu.VMEM((16, edge, 128), jnp.float32),
        ],
        compiler_params=params(16),
        name="degree",
    )(info, index, tiles)


def degree_stages(info, index, tiles):
    def begin(state):
        own, other = partial_degree(info, index, tiles)
        return own + swap(other)

    def add(total, part):
        for step, n in part:
            total = total[:n] + exchange(total[n:], step)
        return total

    parts = list(zip(REDUCE[0], (4, 2, 1)))
    return {
        1: begin,
        2: lambda total: add(total, parts[:2]),
        3: lambda total: add(total, parts[2:]),
    }


def spread_kernel(info, index0, index1, tiles0, tiles1, *refs):
    pieces, (send0, keep0, send1, keep1, x, acc, buf, sem, piece_sem) = refs[:4], refs[4:]
    core = info[4]
    slots = tiles0.shape[0]

    copies = []
    for chain, (steps, (first, rows)) in enumerate(zip(GATHER, ROWS)):
        for s in range(16):
            at = place(info, steps, (s & 1, s >> 1 & 1, s >> 2 & 1, s >> 3))
            block = at["y"] * 4 + at["z"]
            copies.append(
                pltpu.make_async_copy(
                    pieces[chain * 2 + s // 8].at[s % 8],
                    x.at[pl.ds(block * 2, 2), pl.ds(first, rows), :],
                    piece_sem.at[chain, s],
                )
            )
    for copy in copies:
        copy.start()

    def tile_copy(tiles, base, s):
        return pltpu.make_async_copy(tiles.at[s], buf.at[base + s], sem.at[base + s])

    first, second = index0[96], index1[96]

    def begin0(s, carry):
        tile_copy(tiles0, 0, s).start()
        return carry

    def begin1(s, carry):
        tile_copy(tiles1, slots, s).start()
        return carry

    lax.fori_loop(0, first, begin0, 0)
    lax.fori_loop(0, second, begin1, 0)

    def clear(block, carry):
        acc[block] = jnp.zeros(acc.shape[1:], acc.dtype)
        return carry

    lax.fori_loop(0, acc.shape[0], clear, 0)
    for copy in copies:
        copy.wait()

    def locate(t):
        rel = (t >= first).astype(jnp.int32)
        return t - rel * first, rel

    def arrive(t):
        s, rel = locate(t)
        tile_copy(tiles0, rel * slots, s).wait()

    def multiply(t):
        s, rel = locate(t)
        mine = rel == 0
        target = jnp.where(mine, index0[s], index1[s])
        source = jnp.where(mine, index0[48 + s], index1[48 + s])
        acc[target] += jnp.dot(
            buf[rel * slots + s], x[source * 2 + rel], preferred_element_type=jnp.float32
        )

    def several(group, carry):
        for k in range(UNROLL):
            arrive(group * UNROLL + k)
        for k in range(UNROLL):
            multiply(group * UNROLL + k)
        return carry

    def single(t, carry):
        arrive(t)
        multiply(t)
        return carry

    total = first + second
    groups = lax.div(total, UNROLL)
    lax.fori_loop(0, groups, several, 0)
    lax.fori_loop(groups * UNROLL, total, single, 0)
    for chain, (send, keep) in enumerate(((send0, keep0), (send1, keep1))):
        part = pl.ds(ROWS[chain][0], ROWS[chain][1])
        for s, chip in enumerate(chip_slots(info, REDUCE[chain])):
            for rel in range(2):
                block = chip * 2 + (core if rel == 0 else 1 - core)
                if s < 4:
                    keep[s, rel] = acc[block, part, :].astype(jnp.bfloat16)
                else:
                    send[s - 4, rel] = acc[block, part, :].astype(jnp.bfloat16)


def spread(info, work, pieces):
    (index0, tiles0), (index1, tiles1) = work
    slots, edge, _ = tiles0.shape
    return pl.pallas_call(
        spread_kernel,
        out_shape=[
            jax.ShapeDtypeStruct((4, 2, rows, 256), dtype)
            for _, rows in ROWS
            for dtype in (jnp.bfloat16, jnp.bfloat16)
        ],
        in_specs=[SMEM] * 3 + [ANY] * 6,
        out_specs=[VMEM] * 4,
        scratch_shapes=[
            pltpu.VMEM((32, edge, 256), jnp.bfloat16),
            pltpu.VMEM((16, edge, 256), jnp.float32),
            pltpu.VMEM((2 * slots, edge, edge), jnp.bfloat16),
            pltpu.SemaphoreType.DMA((2 * slots,)),
            pltpu.SemaphoreType.DMA((2, 16)),
        ],
        compiler_params=params(56),
        cost_estimate=pl.CostEstimate(
            flops=2 * 47 * edge * edge * 512, bytes_accessed=20 * MIB, transcendentals=0
        ),
        name="spread",
    )(info, index0, index1, tiles0, tiles1, *pieces)


def join_kernel(keep, got, send, rest):
    n = rest.shape[0]
    for s in range(2 * n):
        total = keep[s].astype(jnp.float32) + got[s].astype(jnp.float32)
        if s < n:
            rest[s] = total
        else:
            send[s - n] = total.astype(jnp.bfloat16)


def join(keep, got):
    shape = (keep.shape[0] // 2,) + keep.shape[1:]
    return pl.pallas_call(
        join_kernel,
        out_shape=[
            jax.ShapeDtypeStruct(shape, jnp.bfloat16),
            jax.ShapeDtypeStruct(shape, jnp.float32),
        ],
        in_specs=[VMEM] * 2,
        out_specs=[VMEM] * 2,
        compiler_params=params(16),
        name="join",
    )(keep, got)


def last_join_kernel(keep0, got0, keep1, got1, own, other):
    for chain, (keep, got) in enumerate(((keep0, got0), (keep1, got1))):
        part = pl.ds(ROWS[chain][0], ROWS[chain][1])
        own[part, :] = keep[0, 0] + got[0, 0].astype(jnp.float32)
        other[part, :] = keep[0, 1] + got[0, 1].astype(jnp.float32)


def last_join(keep0, got0, keep1, got1):
    edge = keep0.shape[2] + keep1.shape[2]
    return pl.pallas_call(
        last_join_kernel,
        out_shape=[jax.ShapeDtypeStruct((edge, 256), jnp.float32)] * 2,
        in_specs=[VMEM] * 4,
        out_specs=[VMEM] * 2,
        compiler_params=params(16),
        name="last_join",
    )(keep0, got0, keep1, got1)


def aggregate(info, work, own_half, arrived, stages, state):
    def beside(k, values, state):
        if k not in stages:
            return values, state
        return lax.optimization_barrier((values, stages[k](state)))

    pair = jnp.stack([own_half, arrived])
    have = [pair[None, :, first : first + rows] for first, rows in ROWS]
    for k in range(4):
        got = [exchange(h, steps[k]) for h, steps in zip(have, GATHER)]
        got, state = beside(k, got, state)
        if k < 3:
            have = [jnp.concatenate([h, g]) for h, g in zip(have, got)]
            have = lax.optimization_barrier(have)
    parts = spread(info, work, (have[0], got[0], have[1], got[1]))
    parts, state = beside(4, parts, state)
    send, keep = [parts[0], parts[2]], [parts[1], parts[3]]
    for k in range(2):
        arrived = [exchange(send[chain], REDUCE[chain][k]) for chain in range(2)]
        if 5 + k in stages:
            state = stages[5 + k](state)
        if k == 1 and "after" in stages:
            state, arrived[1] = lax.optimization_barrier((state, arrived[1]))
            state = stages["after"](state)
        arrived, state = lax.optimization_barrier((arrived, state))
        for chain in range(2):
            send[chain], keep[chain] = join(keep[chain], arrived[chain])
        send, state = lax.optimization_barrier((send, state))
    arrived = [exchange(send[chain], REDUCE[chain][2]) for chain in range(2)]
    arrived, state = beside(7, arrived, state)
    own, other = last_join(keep[0], arrived[0], keep[1], arrived[1])
    return own, swap(other), state


def whole_width(core, own, got):
    first = core == 0
    return jnp.concatenate([jnp.where(first, own, got), jnp.where(first, got, own)], axis=1)


def dense_kernel(
    info, features, cotangent, w_self, w_neigh, degree, own, got, output, grad_pre, mean, mine, theirs
):
    deg = degree[:, 0:1]
    core = info[4]
    summed = whole_width(core, own[...], got[...])
    neighbor_mean = (summed / deg).astype(jnp.bfloat16)
    mean[...] = neighbor_mean
    preact = jnp.dot(features[...], w_self[...], preferred_element_type=jnp.float32) + jnp.dot(
        neighbor_mean, w_neigh[...], preferred_element_type=jnp.float32
    )
    part = jax.nn.sigmoid(preact)
    output[...] = (preact * part).astype(jnp.bfloat16)
    grad = (
        cotangent[...].astype(jnp.float32) * part * (1.0 + preact * (1.0 - part))
    ).astype(jnp.bfloat16)
    grad_pre[...] = grad
    back = (
        lax.dot_general(grad, w_neigh[...], CONTRACT_COLS, preferred_element_type=jnp.float32)
        / deg
    )
    mine[...] = jnp.where(core == 0, back[:, :256], back[:, 256:]).astype(jnp.bfloat16)
    theirs[...] = jnp.where(core == 0, back[:, 256:], back[:, :256]).astype(jnp.bfloat16)


def dense(info, features, cotangent, w_self, w_neigh, degree, own, got):
    nodes, width = features.shape
    full = jax.ShapeDtypeStruct((nodes, width), jnp.bfloat16)
    half = jax.ShapeDtypeStruct((nodes, 256), jnp.bfloat16)
    return pl.pallas_call(
        dense_kernel,
        out_shape=[full] * 3 + [half] * 2,
        in_specs=[SMEM] + [VMEM] * 7,
        out_specs=[VMEM] * 5,
        compiler_params=params(24),
        name="dense",
    )(info, features, cotangent, w_self, w_neigh, degree, own, got)


def weights_kernel(info, features, mean, grad_pre, w_self, keep, send, own):
    grad = grad_pre[...]
    grad_self = lax.dot_general(
        features[...], grad, CONTRACT_ROWS, preferred_element_type=jnp.float32
    )
    grad_neigh = lax.dot_general(
        mean[...], grad, CONTRACT_ROWS, preferred_element_type=jnp.float32
    )
    first = info[4] == 0
    keep[...] = jnp.where(first, grad_self, grad_neigh)
    send[...] = jnp.where(first, grad_neigh, grad_self)
    own[...] = lax.dot_general(
        grad, w_self[...], CONTRACT_COLS, preferred_element_type=jnp.float32
    )


def weights(info, features, mean, grad_pre, w_self):
    nodes, width = features.shape
    square = jax.ShapeDtypeStruct((width, width), jnp.float32)
    return pl.pallas_call(
        weights_kernel,
        out_shape=[square, square, jax.ShapeDtypeStruct((nodes, width), jnp.float32)],
        in_specs=[SMEM] + [VMEM] * 4,
        out_specs=[VMEM] * 3,
        compiler_params=params(24),
        name="weights",
    )(info, features, mean, grad_pre, w_self)


def weight_blocks_kernel(info, keep, got, send, rest):
    for s, chip in enumerate(chip_slots(info, REDUCE[0])):
        rows = pl.ds(pl.multiple_of(chip * 64, 64), 64)
        total = keep[rows, :] + got[rows, :]
        if s < 4:
            rest[s] = total
        else:
            send[s - 4] = total


def weight_blocks(info, keep, got):
    shape = jax.ShapeDtypeStruct((4, 64, keep.shape[1]), jnp.float32)
    return pl.pallas_call(
        weight_blocks_kernel,
        out_shape=[shape] * 2,
        in_specs=[SMEM, VMEM, VMEM],
        out_specs=[VMEM] * 2,
        compiler_params=params(16),
        name="weight_blocks",
    )(info, keep, got)


def weight_stages(info, features, w_self):
    steps = REDUCE[0]

    def local(state):
        grad_pre, mean = state
        keep, send, own_term = weights(info, features, mean, grad_pre, w_self)
        return keep, swap(send), own_term

    def first(state):
        keep, got, own_term = state
        send, rest = weight_blocks(info, keep, got)
        return rest + exchange(send, steps[0]), own_term

    def halve(step):
        def stage(state):
            total, own_term = state
            half = total.shape[0] // 2
            return total[:half] + exchange(total[half:], step), own_term

        return stage

    def row_sum(*chosen):
        def stage(state):
            total, own_term = state
            for step in chosen:
                total = total + exchange(total, step)
            return total, own_term

        return stage

    def collect(*chosen):
        def stage(state):
            total, own_term = state
            for step in chosen:
                total = jnp.concatenate([total, exchange(total, step)])
            return total, own_term

        return stage

    def others(total, axis):
        return [exchange(total, (axis, mask, mask)) for mask in (1, 2, 3)]

    def sum_y(state):
        total, own_term = state
        first, second, third = others(total, "y")
        return (total + first) + (second + third), own_term

    def collect_x(state):
        total, own_term = state
        return jnp.concatenate([total] + others(total, "x")), own_term

    return {
        0: local,
        1: first,
        2: halve(steps[1]),
        3: halve(steps[2]),
        4: sum_y,
        5: row_sum(ROW_SUM[2]),
        6: row_sum(ROW_SUM[3]),
        "after": collect(steps[2]),
        7: collect_x,
    }


def both_weights_kernel(info, mine, theirs, grad_self, grad_neigh):
    core = info[4]
    for value, owner in ((mine, core), (theirs, 1 - core)):
        for s in range(8):
            chip = lax.bitwise_xor(info[2], s // 2) * 2 + lax.bitwise_xor(info[3], s % 2)
            rows = pl.ds(pl.multiple_of(chip * 64, 64), 64)

            @pl.when(owner == 0)
            def _(value=value, s=s, rows=rows):
                grad_self[rows, :] = value[s]

            @pl.when(owner == 1)
            def _(value=value, s=s, rows=rows):
                grad_neigh[rows, :] = value[s]


def both_weights(info, total):
    width = total.shape[2]
    return pl.pallas_call(
        both_weights_kernel,
        out_shape=[jax.ShapeDtypeStruct((8 * total.shape[1], width), jnp.float32)] * 2,
        in_specs=[SMEM, VMEM, VMEM],
        out_specs=[VMEM] * 2,
        compiler_params=params(16),
        name="both_weights",
    )(info, total, swap(total))


def finish_kernel(info, own_term, own, got, out):
    out[...] = (own_term[...] + whole_width(info[4], own[...], got[...])).astype(jnp.bfloat16)


def finish(info, own_term, own, got):
    return pl.pallas_call(
        finish_kernel,
        out_shape=jax.ShapeDtypeStruct(own_term.shape, jnp.bfloat16),
        in_specs=[SMEM] + [VMEM] * 3,
        out_specs=VMEM,
        compiler_params=params(16),
        name="finish",
    )(info, own_term, own, got)


def shards(features, w_self, w_neigh, cotangent, tile_values, tile_dst, tile_src, tile_count):
    row, col = lax.axis_index("row"), lax.axis_index("col")
    core = col % 2
    info = jnp.stack([row // 4, row % 4, col // 4, col // 2 % 2, core]).astype(jnp.int32)
    index = jnp.concatenate([tile_dst, tile_src, tile_count])
    first = core == 0
    mine = jnp.where(first, features[:, :256], features[:, 256:])
    theirs = jnp.where(first, features[:, 256:], features[:, :256])
    theirs = swap(theirs)
    theirs, tiles = lax.optimization_barrier((theirs, tile_values))
    work = ((index, tile_values), (swap(index), swap(tiles)))
    own, got, degree = aggregate(
        info, work, mine, theirs, degree_stages(info, index, tile_values), None
    )
    degree = jnp.broadcast_to(degree[0, 0][:, None], (degree.shape[-1], 128))
    output, grad_pre, mean, mine, theirs = dense(
        info, features, cotangent, w_self, w_neigh, degree, own, got
    )
    own, got, (total, own_term) = aggregate(
        info, work, mine, swap(theirs), weight_stages(info, features, w_self), (grad_pre, mean)
    )
    grad_self, grad_neigh = both_weights(info, total)
    grad_features = finish(info, own_term, own, got)
    return (output, grad_features, grad_self, grad_neigh)


def solution(mesh):
    return jax.shard_map(
        shards,
        mesh=mesh,
        in_specs=(
            P(("row", "col"), None),
            P(),
            P(),
            P(("row", "col"), None),
            P(("row", "col"), None, None),
            P(("row", "col")),
            P(("row", "col")),
            P(("row", "col")),
        ),
        out_specs=(P(("row", "col"), None), P(("row", "col"), None), P(), P()),
        check_vma=False,
    )
```
